128 devices in a mesh: section: 4 (over x), dp: 16 (over z, y), mp: 2 (over core).
Axes of the slice: x: 4, y: 4, z: 4, core: 2. Of those that a mesh axis runs over, the one named last changes fastest.
Arguments:
- tokens: bfloat16 [128, 8192], P(None, 'dp'), may hold values from -13 to 13
- keep: int32 [4, 128], replicated, may hold values 0 or 1
- norm_gain: bfloat16 [4, 8192], P('section', 'dp'), may hold values from 0.25 to 1.75
- w_up: bfloat16 [4, 8192, 14336], P('section', 'dp', 'mp'), may hold values from -0.0625 to 0.0625
- w_down: bfloat16 [4, 14336, 8192], P('section', 'mp', 'dp'), may hold values from -0.09375 to 0.09375
- head_gain: bfloat16 [8192], P('dp'), may hold values from 0.25 to 1.75
- w_head: bfloat16 [8192, 65536], P('dp', ('section', 'mp')), may hold values from -2 to 2
- exit_idx: int32 [4, 32], replicated, may hold values from 0 to 127
- exit_count: int32 [4], replicated, may hold values from 1 to 32, 80 in all
- kl_bucket: int32 [4, 32], replicated, may hold values from 0 to 15
Outputs:
- feature_grad: float32 [128, 8192], P(('section', 'mp'), 'dp')
- kl_rows: float32 [128], P('dp')
- histogram: float32 [4, 16], replicated
The draws below stay inside these ranges and needn't reach their ends.
Inputs may be any that keep to these rules, and one draw needn't show every extreme that they name: Section s's live exits are the first exit_count[s] slots of row s; the largest count equals 32.
All inputs are finite; a program needn't handle non-finite values.
Results may differ from the reference program's by a relative error of at most 0.03405.
Values may be sent and summed in bfloat16 or wider, within the bound.
No kernel may reach another device: no remote copies, remote signals or barrier semaphores. Data moves between devices by JAX's collectives and lax.ppermute only.
A program may use at most 128 MiB of HBM per device.

```python
import math
import jax
import jax.numpy as jnp
import numpy as np
from jax import lax

D = 8192
FF = 14336
V = 65536
TOK = 128
XS = 32
NB = 16
N_SECTION = 4


def common_direction(key):
    return jnp.clip(jax.random.normal(key, (D,), jnp.float32), -3.0, 3.0)


def draw_tokens(key, part):
    direction = common_direction(key)
    key = jax.random.fold_in(key, 11)
    noise_key, strength_key, pick_key = jax.random.split(key, 3)
    noise = jnp.clip(jax.random.normal(noise_key, (TOK, D), jnp.float32), -4.0, 4.0)
    strength = jnp.exp(jax.random.uniform(strength_key, (TOK,), jnp.float32, math.log(0.5), math.log(3.0)))
    portion = 0.35
    chosen = jnp.where(jax.random.uniform(pick_key, (TOK,), jnp.float32) < portion, strength, 0.0)
    return (noise + chosen[:, None] * direction[None, :]).astype(jnp.bfloat16)


def draw_w_head(key, part):
    direction = common_direction(key)
    key = jax.random.fold_in(key, 23)
    base_key, spot_key = jax.random.split(key, 2)
    base_scale = (D // 9) ** (-0.5)
    base = jnp.clip(jax.random.normal(base_key, (D, V), jnp.float32), -4.0, 4.0) * base_scale
    strength = 300.0
    spots = jax.random.permutation(spot_key, V)[:4]
    levels = strength - 2.0 * jnp.arange(4, dtype=jnp.float32)
    column_hit = (jnp.arange(V)[:, None] == spots[None, :]).astype(jnp.float32)
    lifted = jnp.sum(column_hit * levels[None, :], axis=1)
    return (base + direction[:, None] * lifted[None, :] / D).astype(jnp.bfloat16)


def touch_ends(values, rng, smallest, top_value):
    place = [jax.random.randint(jax.random.fold_in(rng, axis), (), 0, length) for axis, length in enumerate(values.shape)]
    longest = values.shape.index(max(values.shape))
    beside = place[:longest] + [(place[longest] + 1) % values.shape[longest]] + place[longest + 1:]
    return values.at[tuple(place)].set(smallest).at[tuple(beside)].set(top_value)


def block_scale(key, extent, shards, least, high):
    loudness, own = 1.0, jax.random.fold_in(key, 6)
    for axis_at, shards_of in shards:
        steps = jnp.exp(jax.random.uniform(jax.random.fold_in(own, axis_at), (shards_of,), jnp.float32, least / len(shards), high / len(shards)))
        loudness = loudness * jnp.repeat(steps, extent[axis_at] // shards_of).reshape([-1 if axis == axis_at else 1 for axis in range(len(extent))])
    return loudness


def length_profile(count, total, bound, skew):
    portions = [(1 << 20) // math.isqrt(standing ** skew) + 1 for standing in range(2, count + 1)]
    spare, given = total - bound - (count - 1), [1] * (count - 1)
    while spare > 0:
        free = [i for i in range(count - 1) if given[i] < bound]
        pool, left = sum([portions[i] for i in free]), spare
        for i in free:
            extra = min(bound - given[i], max(1, left * portions[i] // pool), spare)
            given[i] = given[i] + extra
            spare = spare - extra
    return np.array([bound] + given)


def ragged(rng, number_of, total, limit, skew):
    if number_of == 2:
        one = jax.random.randint(rng, (), max(1, total - limit), min(limit, total - 1) + 1)
        return jnp.stack([one, total - one])
    lengths = jnp.asarray(length_profile(number_of, total, limit, skew), jnp.int32)
    twos = (number_of - 1) // 2
    giver, taker = lengths[1:1 + 2 * twos:2], lengths[2:2 + 2 * twos:2]
    margin = jnp.minimum(giver - 1, limit - taker)
    passed = jax.random.randint(jax.random.fold_in(rng, 1), (twos,), 0, 1 << 20) % (margin + 1)
    lengths = lengths.at[1:1 + 2 * twos:2].set(giver - passed).at[2:2 + 2 * twos:2].set(taker + passed)
    return lengths[jax.random.permutation(jax.random.fold_in(rng, 2), number_of)]


def centred(key, extent, scale, most, pieces=(), kind=jnp.bfloat16):
    result = scale * jax.random.normal(key, extent, jnp.float32)
    if pieces:
        result = result * block_scale(key, extent, pieces, -0.22, 0.18)
    return jnp.clip(result, -most, most).astype(kind)


def setup_inputs(seed: int = 0) -> dict:
    streams_of = jax.random.split(jax.random.key(seed), 11)
    return {
        "tokens": draw_tokens(jax.random.fold_in(streams_of[10], 71), 0),
        "keep": touch_ends((jax.random.randint(streams_of[1], (N_SECTION, TOK), 0, 4) < 3).astype(jnp.int32), jax.random.fold_in(streams_of[1], 1), 0, 1),
        "norm_gain": jnp.clip(1.0 + 0.15 * jax.random.normal(streams_of[2], (N_SECTION, D), jnp.float32), 0.25, 1.75).astype(jnp.bfloat16),
        "w_up": centred(streams_of[3], (N_SECTION, D, FF), D ** -0.5, 0.0625, ((0, 4), (1, 16), (2, 2))),
        "w_down": centred(streams_of[4], (N_SECTION, FF, D), (FF // 4) ** -0.5, 0.09375, ((0, 4), (1, 2), (2, 16))),
        "head_gain": jnp.clip(1.0 + 0.15 * jax.random.normal(streams_of[5], (D,), jnp.float32), 0.25, 1.75).astype(jnp.bfloat16),
        "w_head": draw_w_head(jax.random.fold_in(streams_of[10], 71), 0),
        "exit_idx": touch_ends(jax.random.randint(streams_of[7], (N_SECTION, XS), 0, TOK), jax.random.fold_in(streams_of[7], 1), 0, TOK - 1).astype(jnp.int32),
        "exit_count": ragged(streams_of[8], N_SECTION, 5 * XS // 2, XS, 2).astype(jnp.int32),
        "kl_bucket": touch_ends(jax.random.randint(streams_of[9], (N_SECTION, XS), 0, NB), jax.random.fold_in(streams_of[9], 1), 0, NB - 1).astype(jnp.int32),
    }


epsilon = 1e-05

def row_scale(values):
    return lax.rsqrt(lax.optimization_barrier(jnp.mean(values * values, axis=-1)) + epsilon)

def head_logits(rows, head_gain, w_head):
    wide = rows.astype(jnp.float32)
    scale = row_scale(wide)
    normed = (wide * head_gain.astype(jnp.float32)).astype(jnp.bfloat16)
    logits = jnp.dot(normed, w_head, preferred_element_type=jnp.float32) * scale[:, None]
    return (logits, scale)

def log_total(logits):
    peak = lax.optimization_barrier(jnp.max(logits, axis=-1))
    return peak + jnp.log(lax.optimization_barrier(jnp.sum(jnp.exp(logits - peak[:, None]), axis=-1)))

def reference(tokens, keep, norm_gain, w_up, w_down, head_gain, w_head, exit_idx, exit_count, kl_bucket):
    state = tokens
    states = []
    for section in range(N_SECTION):
        wide = state.astype(jnp.float32)
        scale = row_scale(wide)
        normed = (wide * norm_gain[section].astype(jnp.float32)).astype(jnp.bfloat16)
        raised = jnp.dot(normed, w_up[section], preferred_element_type=jnp.float32) * scale[:, None]
        active = jax.nn.silu(raised).astype(jnp.bfloat16)
        lowered = jnp.dot(active, w_down[section], preferred_element_type=jnp.float32)
        state = (wide + keep[section][:, None].astype(jnp.float32) * lowered).astype(jnp.bfloat16)
        states.append(state)
    exits = jnp.concatenate([jnp.take(states[which], exit_idx[which], axis=0) for which in range(N_SECTION)], axis=0)
    finals = jnp.take(state, exit_idx.reshape(-1), axis=0)
    exit_logits, exit_scale = head_logits(exits, head_gain, w_head)
    final_logits, final_scale = head_logits(finals, head_gain, w_head)
    exit_total = log_total(exit_logits)
    final_total = log_total(final_logits)
    exit_prob = jnp.exp(exit_logits - exit_total[:, None])
    final_prob = jnp.exp(final_logits - final_total[:, None])
    live = (jnp.arange(XS)[None, :] < exit_count[:, None]).reshape(-1).astype(jnp.float32)
    kl_rows = (lax.optimization_barrier(jnp.sum(final_prob * (final_logits - exit_logits), axis=-1)) - final_total + exit_total) * live
    gap = ((exit_prob - final_prob) * live[:, None]).astype(jnp.bfloat16)
    feature_grad = jnp.dot(gap, w_head.T, preferred_element_type=jnp.float32) * exit_scale[:, None]
    bucket_hot = (kl_bucket[:, :, None] == jnp.arange(NB)[None, None, :]).astype(jnp.float32)
    histogram = jnp.einsum('si,sib->sb', kl_rows.reshape(N_SECTION, XS), bucket_hot, precision=lax.Precision.HIGHEST)
    return (feature_grad, kl_rows, histogram)
```

```python
import jax
import jax.numpy as jnp
from jax import lax
from jax.experimental import pallas as pl
from jax.experimental.pallas import tpu as pltpu
from jax.sharding import PartitionSpec as P

D = 8192
XS = 32
NB = 16
LIVE = 80
DP = 16
PAIRS = LIVE // DP
HALF = LIVE // 2
FB = 896
NF = 8
COLS = 8192
TILES = COLS // 128
EPS = 1e-05
f32 = jnp.float32
bf16 = jnp.bfloat16
VMEM_LIMIT = 56 * 1024 * 1024


def call(kernel, out_shape, **kw):
    return pl.pallas_call(
        kernel,
        out_shape=out_shape,
        compiler_params=pltpu.CompilerParams(vmem_limit_bytes=VMEM_LIMIT),
        **kw,
    )


def iota(shape, dim):
    return lax.broadcasted_iota(jnp.int32, shape, dim)


def split_sum(column):
    high = column.astype(bf16).astype(f32)
    return high, (column - high).astype(bf16).astype(f32)


def prep_kernel(count, index, keep, tokens, rows, kept, section, slots):
    lane = iota((1, 4 * XS), 1)
    own = lane // XS
    place = lane % XS
    start = jnp.int32(0)
    position = jnp.full((1, 4 * XS), -1, jnp.int32)
    for s in range(4):
        inside = (own == s) & (place < count[s])
        position = jnp.where(inside, place + start, position)
        start = start + count[s]
    hit = iota((LIVE, 4 * XS), 0) == position
    pick = jnp.where(hit, 1.0, 0.0)
    token = jnp.sum(pick * index[...].astype(f32), axis=1, keepdims=True).astype(jnp.int32)
    chosen = jnp.where(iota((LIVE, 128), 1) == token, 1.0, 0.0)
    rows[...] = jnp.dot(chosen.astype(bf16), tokens[...], preferred_element_type=f32).astype(bf16)
    flag = jnp.sum(chosen * keep[...].astype(f32), axis=1, keepdims=True)
    kept[...] = jnp.broadcast_to(flag, kept.shape)
    which = jnp.sum(pick * own.astype(f32), axis=1, keepdims=True)
    section[...] = jnp.broadcast_to(which, section.shape)
    slots[...] = pick


def up_kernel(state, gain, weight, out):
    wide = state[...].astype(f32)
    normed = (wide * gain[...].astype(f32)).astype(bf16)
    high, low = split_sum(jnp.sum(wide * wide, axis=1, keepdims=True))
    lane = iota((LIVE, 128), 1)
    extra = jnp.where(lane == 0, high, jnp.where(lane == 1, low, 0.0))
    part = jnp.dot(normed, weight[...], preferred_element_type=f32)
    for t in range(2):
        out[t, 0, :, :FB] = part[t * HALF : (t + 1) * HALF].astype(bf16)
        out[t, 0, :, FB:] = extra[t * HALF : (t + 1) * HALF].astype(bf16)


def mid_kernel(parts, out):
    total = parts[0].astype(f32)
    for j in range(1, DP):
        total = total + parts[j].astype(f32)
    scale = lax.rsqrt((total[:, FB : FB + 1] + total[:, FB + 1 : FB + 2]) / D + EPS)
    active = jax.nn.silu(total[:, :FB] * scale).astype(bf16)
    for j in range(DP):
        out[j] = active


def down_kernel(active, weight, kept, out):
    step = pl.program_id(0)
    both = jnp.concatenate([active[0, 0].astype(f32), active[1, 0].astype(f32)], axis=0)
    part = jnp.dot(both.astype(bf16), weight[...], preferred_element_type=f32)

    @pl.when(step == 0)
    def _():
        out[...] = part

    @pl.when(step > 0)
    def _():
        out[...] = out[...] + part

    @pl.when(step == NF - 1)
    def _():
        out[...] = out[...] * kept[:, :1]


def head_kernel(exits, finals, gain, weight, out):
    step = pl.program_id(0)
    wide = jnp.concatenate([exits[...].astype(f32), finals[...].astype(f32)], axis=0)
    headed = (wide * gain[...].astype(f32)).astype(bf16)
    part = jnp.dot(headed, weight[...], preferred_element_type=f32)
    tiles = part.reshape(2 * LIVE, 8, 128)
    base = pl.multiple_of(step * 8, 8)
    for i in range(DP):
        for kind in range(2):
            for p in range(PAIRS):
                slot = kind * PAIRS + p
                out[i, pl.ds(slot * TILES + base, 8), :] = tiles[kind * LIVE + i * PAIRS + p]

    @pl.when(step == 0)
    def _():
        squares = jnp.broadcast_to(jnp.sum(wide * wide, axis=1, keepdims=True), (2 * LIVE, 128))
        for i in range(DP):
            for kind in range(2):
                at = kind * LIVE + i * PAIRS
                first = 2 * PAIRS * TILES + kind * 8
                out[i, first : first + PAIRS, :] = squares[at : at + PAIRS]
                out[i, first + PAIRS : first + 8, :] = jnp.zeros((8 - PAIRS, 128), f32)


def peak_kernel(parts, logits, stats, total):
    step = pl.program_id(0)

    @pl.when(step == 0)
    def _():
        total[...] = parts[0]

    @pl.when(step > 0)
    def _():
        total[...] = total[...] + parts[0]

    @pl.when(step == DP - 1)
    def _():
        lane = iota((1, 128), 1)
        for p in range(PAIRS):
            z = []
            for kind in range(2):
                at = 2 * PAIRS * TILES + kind * 8 + p
                scale = lax.rsqrt(total[at : at + 1, :] / D + EPS)
                first = (kind * PAIRS + p) * TILES
                value = total[first : first + TILES, :] * scale
                logits[first : first + TILES, :] = value
                z.append(value)
                if kind == 0:
                    exit_scale = scale
            entries = []
            for value in z:
                peak = jnp.max(jnp.max(value, axis=0, keepdims=True), axis=1, keepdims=True)
                power = jnp.exp(value - peak)
                entries += [peak, jnp.sum(jnp.sum(power, axis=0, keepdims=True), axis=1, keepdims=True)]
            cross = power * (z[1] - z[0])
            entries.append(jnp.sum(jnp.sum(cross, axis=0, keepdims=True), axis=1, keepdims=True))
            entries.append(exit_scale)
            row = jnp.zeros((1, 128), f32)
            for n, entry in enumerate(entries):
                row = jnp.where(lane == n, entry, row)
            for j in range(8):
                stats[j, p : p + 1, :] = row
        for j in range(8):
            stats[j, PAIRS:, :] = jnp.ones((8 - PAIRS, 128), f32)


def gap_kernel(logits, stats, out):
    everyone = stats[...]
    lane = iota((1, 128), 1)
    peaks = jnp.max(everyone, axis=0)
    marks = []
    for column in (0, 2):
        peak = peaks[:, column : column + 1]
        weight = jnp.exp(everyone[:, :, column : column + 1] - peak[None])
        total = jnp.sum(weight * everyone[:, :, column + 1 : column + 2], axis=0)
        marks.append((peak + jnp.log(total), weight, total))
    (log_exit, _, _), (log_final, weight, total) = marks
    cross = jnp.sum(weight * everyone[:, :, 4:5], axis=0)
    kl = cross / total - log_final + log_exit
    exit_scale = peaks[:, 5:6]
    for p in range(PAIRS):
        ze = logits[p * TILES : (p + 1) * TILES, :]
        zf = logits[(PAIRS + p) * TILES : (PAIRS + p + 1) * TILES, :]
        gap = jnp.exp(ze - log_exit[p : p + 1]) - jnp.exp(zf - log_final[p : p + 1])
        gap = (gap * exit_scale[p : p + 1]).astype(bf16)
        for j in range(DP):
            out[j, p * TILES : (p + 1) * TILES, :] = gap
    high, rest = split_sum(kl)
    middle = (kl - high).astype(bf16).astype(f32)
    low = kl - high - middle
    lanes = iota((8, 128), 1)
    carried = jnp.where(lanes == 0, high, jnp.where(lanes == 1, middle, jnp.where(lanes == 2, low, 0.0)))
    extra = jnp.concatenate([carried, jnp.zeros((8, 128), f32)], axis=0).astype(bf16)
    for j in range(DP):
        out[j, PAIRS * TILES :, :] = extra


def grad_kernel(gaps, weight, slots, buckets, out, kl_out, hist, total):
    step = pl.program_id(0)
    base = pl.multiple_of(step * 16, 16)
    rows = [gaps[:, pl.ds(p * TILES + base, 16), :].astype(f32) for p in range(PAIRS)]
    left = jnp.stack(rows, axis=1).reshape(LIVE, 16 * 128).astype(bf16)
    part = lax.dot_general(left, weight[...], (((1,), (1,)), ((), ())), preferred_element_type=f32)

    @pl.when(step == 0)
    def _():
        total[...] = part

    @pl.when(step > 0)
    def _():
        total[...] = total[...] + part

    @pl.when(step == 3)
    def _():
        pick = slots[...]
        out[...] = lax.dot_general(
            pick.astype(bf16),
            total[...].astype(bf16),
            (((0,), (0,)), ((), ())),
            preferred_element_type=f32,
        ).astype(bf16)
        extra = gaps[:, PAIRS * TILES :, :].astype(f32)[:, :PAIRS, :].reshape(LIVE, 128)
        kl = jnp.sum(extra, axis=1, keepdims=True)
        by_slot = jnp.sum(pick * kl, axis=0, keepdims=True)
        kl_out[...] = jnp.broadcast_to(by_slot, (8, 128))
        mine = jnp.where(iota((8, 128), 1) // XS == iota((8, 128), 0), by_slot, 0.0)
        hot = jnp.where(iota((NB, 128), 0) == buckets[...], 1.0, 0.0)
        hist[...] = lax.dot_general(
            mine,
            hot,
            (((1,), (1,)), ((), ())),
            preferred_element_type=f32,
            precision=lax.Precision.HIGHEST,
        )


def exchange(value, axis):
    return lax.all_to_all(value, axis, 0, 0)


def shards(
    tokens, keep, norm_gain, w_up, w_down, head_gain, w_head, exit_idx, exit_count, kl_bucket
):
    sections = lax.axis_size("section")
    section_id = lax.axis_index("section")
    up_local = w_up[0]
    down_local = w_down[0]
    keep_mine = lax.dynamic_slice_in_dim(keep, section_id, 1, 0)
    shape = jax.ShapeDtypeStruct
    vmem = pl.BlockSpec(memory_space=pltpu.VMEM)
    current, kept, section_of, slots = call(
        prep_kernel,
        (
            shape((LIVE, 512), bf16),
            shape((LIVE, 128), f32),
            shape((LIVE, 128), f32),
            shape((LIVE, 128), f32),
        ),
        in_specs=[pl.BlockSpec(memory_space=pltpu.SMEM), vmem, vmem, vmem],
        out_specs=[vmem] * 4,
    )(exit_count, exit_idx.reshape(1, -1), keep_mine, tokens)
    mine = current
    for step in range(sections):
        parts = call(
            up_kernel,
            shape((2, NF, HALF, FB + 128), bf16),
            grid=(NF,),
            in_specs=[
                pl.BlockSpec((LIVE, 512), lambda f: (0, 0)),
                pl.BlockSpec((1, 512), lambda f: (0, 0)),
                pl.BlockSpec((512, FB), lambda f: (0, f)),
            ],
            out_specs=pl.BlockSpec((2, 1, HALF, FB + 128), lambda f: (0, f, 0, 0)),
        )(current, norm_gain, up_local)
        parts = exchange(parts.reshape(DP, HALF, FB + 128), "dp")
        active = call(
            mid_kernel, shape((DP, HALF, FB), bf16), in_specs=[vmem], out_specs=vmem
        )(parts)
        active = exchange(active, "dp")
        lowered = call(
            down_kernel,
            shape((LIVE, 512), f32),
            grid=(NF,),
            in_specs=[
                pl.BlockSpec((2, 1, HALF, FB), lambda f: (0, f, 0, 0)),
                pl.BlockSpec((FB, 512), lambda f: (f, 0)),
                pl.BlockSpec((LIVE, 128), lambda f: (0, 0)),
            ],
            out_specs=pl.BlockSpec((LIVE, 512), lambda f: (0, 0)),
        )(active.reshape(2, NF, HALF, FB), down_local, kept)
        other = lax.ppermute(lowered, "mp", [(0, 1), (1, 0)])
        result = (current.astype(f32) + (lowered + other)).astype(bf16)
        mine = jnp.where(section_id == step, result, mine)
        if step < sections - 1:
            current = lax.ppermute(result, "section", [(i, i + 1) for i in range(sections - 1)])
    zero = jnp.zeros_like(mine)
    own_exit = jnp.where(section_of[:, :1] == section_id.astype(f32), mine, zero)
    own_final = jnp.where(section_id == sections - 1, mine, zero)
    held = jnp.stack([own_exit, own_final])
    spread = held
    for k in range(1, sections):
        spread = spread + lax.ppermute(held, "section", [(i, (i + k) % sections) for i in range(sections)])
    extent = 2 * PAIRS * TILES + 16
    parts = call(
        head_kernel,
        shape((DP, extent, 128), f32),
        grid=(8,),
        in_specs=[
            pl.BlockSpec((LIVE, 512), lambda k: (0, 0)),
            pl.BlockSpec((LIVE, 512), lambda k: (0, 0)),
            pl.BlockSpec((1, 512), lambda k: (0, 0)),
            pl.BlockSpec((512, 1024), lambda k: (0, k)),
        ],
        out_specs=pl.BlockSpec((DP, extent, 128), lambda k: (0, 0, 0)),
    )(spread[0], spread[1], head_gain.reshape(1, -1), w_head)
    parts = exchange(parts, "dp")
    logits, stats = call(
        peak_kernel,
        (shape((2 * PAIRS * TILES, 128), f32), shape((8, 8, 128), f32)),
        grid=(DP,),
        in_specs=[pl.BlockSpec((1, extent, 128), lambda j: (j, 0, 0))],
        out_specs=[
            pl.BlockSpec((2 * PAIRS * TILES, 128), lambda j: (0, 0)),
            pl.BlockSpec((8, 8, 128), lambda j: (0, 0, 0)),
        ],
        scratch_shapes=[pltpu.VMEM((extent, 128), f32)],
    )(parts)
    stats = exchange(stats, ("section", "mp"))
    extent = PAIRS * TILES + 16
    gaps = call(
        gap_kernel, shape((DP, extent, 128), bf16), in_specs=[vmem] * 2, out_specs=vmem
    )(logits, stats)
    gaps = exchange(gaps, "dp")
    feature, kl, hist = call(
        grad_kernel,
        (shape((128, 512), bf16), shape((8, 128), f32), shape((8, NB), f32)),
        grid=(4,),
        in_specs=[
            pl.BlockSpec((DP, extent, 128), lambda k: (0, 0, 0)),
            pl.BlockSpec((512, 2048), lambda k: (0, k)),
            pl.BlockSpec((LIVE, 128), lambda k: (0, 0)),
            pl.BlockSpec((1, 128), lambda k: (0, 0)),
        ],
        out_specs=[
            pl.BlockSpec((128, 512), lambda k: (0, 0)),
            pl.BlockSpec((8, 128), lambda k: (0, 0)),
            pl.BlockSpec((8, NB), lambda k: (0, 0)),
        ],
        scratch_shapes=[pltpu.VMEM((LIVE, 512), f32)],
    )(gaps, w_head, slots, kl_bucket.reshape(1, -1))
    feature = exchange(feature.reshape(8, 16, 512), ("section", "mp"))
    feature_grad = jnp.sum(feature.astype(f32), axis=0)
    kl_here = lax.dynamic_slice_in_dim(kl[0], lax.axis_index("dp") * 8, 8, 0)
    return (feature_grad, kl_here, hist[:4])


def solution(mesh):
    return jax.shard_map(
        shards,
        mesh=mesh,
        in_specs=(
            P(None, "dp"),
            P(),
            P("section", "dp"),
            P("section", "dp", "mp"),
            P("section", "mp", "dp"),
            P("dp"),
            P("dp", ("section", "mp")),
            P(),
            P(),
            P(),
        ),
        out_specs=(P(("section", "mp"), "dp"), P("dp"), P()),
        check_vma=False,
    )
```

```python
import jax
import jax.numpy as jnp
from jax import lax
from jax.experimental import pallas as pl
from jax.experimental.pallas import tpu as pltpu
from jax.sharding import PartitionSpec as P

D = 8192
XS = 32
NB = 16
LIVE = 80
DP = 16
PAIRS = LIVE // DP
HALF = LIVE // 2
FB = 896
NF = 8
COLS = 8192
TILES = COLS // 128
BLOCK = 2048
BLOCKS = COLS // BLOCK
SENDERS = 4
STEPS = 32767.0 / 32768.0
EPS = 1e-05
f32 = jnp.float32
bf16 = jnp.bfloat16
VMEM_LIMIT = 16 * 1024 * 1024


def call(kernel, out_shape, **kw):
    return pl.pallas_call(
        kernel,
        out_shape=out_shape,
        compiler_params=pltpu.CompilerParams(vmem_limit_bytes=VMEM_LIMIT),
        **kw,
    )


def iota(shape, dim):
    return lax.broadcasted_iota(jnp.int32, shape, dim)


def split_sum(column):
    high = column.astype(bf16).astype(f32)
    return high, (column - high).astype(bf16).astype(f32)


def prep_kernel(count, index, keep, tokens, rows, kept, section, slots):
    lane = iota((1, 4 * XS), 1)
    own = lane // XS
    place = lane % XS
    start = jnp.int32(0)
    position = jnp.full((1, 4 * XS), -1, jnp.int32)
    for s in range(4):
        inside = (own == s) & (place < count[s])
        position = jnp.where(inside, place + start, position)
        start = start + count[s]
    hit = iota((LIVE, 4 * XS), 0) == position
    pick = jnp.where(hit, 1.0, 0.0)
    token = jnp.sum(pick * index[...].astype(f32), axis=1, keepdims=True).astype(jnp.int32)
    chosen = jnp.where(iota((LIVE, 128), 1) == token, 1.0, 0.0)
    rows[...] = jnp.dot(chosen.astype(bf16), tokens[...], preferred_element_type=f32).astype(bf16)
    flag = jnp.sum(chosen * keep[...].astype(f32), axis=1, keepdims=True)
    kept[...] = jnp.broadcast_to(flag, kept.shape)
    which = jnp.sum(pick * own.astype(f32), axis=1, keepdims=True)
    section[...] = jnp.broadcast_to(which, section.shape)
    slots[...] = pick


def up_kernel(state, gain, weight, out):
    wide = state[...].astype(f32)
    normed = (wide * gain[...].astype(f32)).astype(bf16)
    high, low = split_sum(jnp.sum(wide * wide, axis=1, keepdims=True))
    lane = iota((LIVE, 128), 1)
    extra = jnp.where(lane == 0, high, jnp.where(lane == 1, low, 0.0))
    for f in range(NF):
        part = jnp.dot(normed, weight[:, f * FB : (f + 1) * FB], preferred_element_type=f32)
        for t in range(2):
            out[t, f, :, :FB] = part[t * HALF : (t + 1) * HALF].astype(bf16)
            out[t, f, :, FB:] = extra[t * HALF : (t + 1) * HALF].astype(bf16)


def mid_kernel(parts, out):
    total = parts[0].astype(f32)
    for j in range(1, DP):
        total = total + parts[j].astype(f32)
    scale = lax.rsqrt((total[:, FB : FB + 1] + total[:, FB + 1 : FB + 2]) / D + EPS)
    active = jax.nn.silu(total[:, :FB] * scale).astype(bf16)
    for j in range(DP):
        out[j] = active


def down_kernel(active, weight, kept, out):
    total = jnp.zeros((LIVE, 512), f32)
    for f in range(NF):
        both = jnp.concatenate([active[0, f].astype(f32), active[1, f].astype(f32)], axis=0)
        total = total + jnp.dot(
            both.astype(bf16), weight[f * FB : (f + 1) * FB, :], preferred_element_type=f32
        )
    out[...] = total * kept[:, :1]


def power_above(value):
    return jnp.ceil(jnp.log2(jnp.maximum(value, 1e-30)))


def head_kernel(exits, finals, gain, weight, out, parts):
    wide = jnp.concatenate([exits[...].astype(f32), finals[...].astype(f32)], axis=0)
    headed = (wide * gain[...].astype(f32)).astype(bf16)
    peak = jnp.zeros((2 * LIVE, BLOCK), f32)
    for k in range(BLOCKS):
        part = jnp.dot(headed, weight[:, k * BLOCK : (k + 1) * BLOCK], preferred_element_type=f32)
        parts[k] = part
        peak = jnp.maximum(peak, jnp.abs(part))
    power = power_above(jnp.max(peak, axis=1, keepdims=True))
    factor = jnp.exp2(15.0 - power) * STEPS
    for k in range(BLOCKS):
        scaled = jnp.clip(jnp.round(parts[k] * factor), -32767.0, 32767.0)
        tiles = scaled.reshape(2 * LIVE, 16, 128).astype(jnp.int32).astype(jnp.int16)
        for i in range(DP):
            for kind in range(2):
                for p in range(PAIRS):
                    first = (kind * PAIRS + p) * TILES + 16 * k
                    out[i, first : first + 16, :] = tiles[kind * LIVE + i * PAIRS + p]
    squares = jnp.sum(wide * wide, axis=1, keepdims=True)
    square_power = power_above(squares)
    whole = jnp.round(squares * jnp.exp2(29.0 - square_power)).astype(jnp.int32)
    lane = iota((2 * LIVE, 128), 1)
    extra = jnp.where(lane == 0, power.astype(jnp.int32), 0)
    extra = jnp.where(lane == 1, whole >> 15, extra)
    extra = jnp.where(lane == 2, whole & 32767, extra)
    extra = jnp.where(lane == 3, square_power.astype(jnp.int32), extra)
    gap = jnp.zeros((8 - PAIRS, 128), jnp.int32)
    for i in range(DP):
        mine = [extra[kind * LIVE + i * PAIRS : kind * LIVE + (i + 1) * PAIRS] for kind in range(2)]
        rows = jnp.concatenate([mine[0], gap, mine[1], gap], axis=0)
        out[i, 2 * PAIRS * TILES :, :] = rows.astype(jnp.int16)


def peak_kernel(parts, logits, stats, total):
    step = pl.program_id(0)

    @pl.when(step == 0)
    def _():
        total[...] = jnp.zeros_like(total)

    sums = []
    for j in range(SENDERS):
        extra = parts[j, 2 * PAIRS * TILES :, :].astype(jnp.int32).astype(f32)
        factor = jnp.exp2(extra[:, 0:1] - 15.0) * (1.0 / STEPS)
        squares = (extra[:, 1:2] * 32768.0 + extra[:, 2:3]) * jnp.exp2(extra[:, 3:4] - 29.0)
        sums.append((factor, squares))
    for slot in range(2 * PAIRS):
        row = slot // PAIRS * 8 + slot % PAIRS
        first = slot * TILES
        value = total[first : first + TILES, :]
        for j in range(SENDERS):
            whole = parts[j, first : first + TILES, :].astype(jnp.int32).astype(f32)
            value = value + whole * sums[j][0][row : row + 1]
        total[first : first + TILES, :] = value
    extra = total[2 * PAIRS * TILES :, :]
    for j in range(SENDERS):
        extra = extra + sums[j][1]
    total[2 * PAIRS * TILES :, :] = extra

    @pl.when(step == DP // SENDERS - 1)
    def _():
        lane = iota((1, 128), 1)
        for p in range(PAIRS):
            z = []
            for kind in range(2):
                at = 2 * PAIRS * TILES + kind * 8 + p
                scale = lax.rsqrt(total[at : at + 1, :] / D + EPS)
                first = (kind * PAIRS + p) * TILES
                value = total[first : first + TILES, :] * scale
                logits[first : first + TILES, :] = value
                z.append(value)
                if kind == 0:
                    exit_scale = scale
            entries = []
            for value in z:
                peak = jnp.max(jnp.max(value, axis=0, keepdims=True), axis=1, keepdims=True)
                power = jnp.exp(value - peak)
                entries += [peak, jnp.sum(jnp.sum(power, axis=0, keepdims=True), axis=1, keepdims=True)]
            cross = power * (z[1] - z[0])
            entries.append(jnp.sum(jnp.sum(cross, axis=0, keepdims=True), axis=1, keepdims=True))
            entries.append(exit_scale)
            row = jnp.zeros((1, 128), f32)
            for n, entry in enumerate(entries):
                row = jnp.where(lane == n, entry, row)
            for j in range(8):
                stats[j, p : p + 1, :] = row
        for j in range(8):
            stats[j, PAIRS:, :] = jnp.ones((8 - PAIRS, 128), f32)


def gap_kernel(logits, stats, out):
    everyone = stats[...]
    lane = iota((1, 128), 1)
    peaks = jnp.max(everyone, axis=0)
    marks = []
    for column in (0, 2):
        peak = peaks[:, column : column + 1]
        weight = jnp.exp(everyone[:, :, column : column + 1] - peak[None])
        total = jnp.sum(weight * everyone[:, :, column + 1 : column + 2], axis=0)
        marks.append((peak + jnp.log(total), weight, total))
    (log_exit, _, _), (log_final, weight, total) = marks
    cross = jnp.sum(weight * everyone[:, :, 4:5], axis=0)
    kl = cross / total - log_final + log_exit
    exit_scale = peaks[:, 5:6]
    for p in range(PAIRS):
        ze = logits[p * TILES : (p + 1) * TILES, :]
        zf = logits[(PAIRS + p) * TILES : (PAIRS + p + 1) * TILES, :]
        gap = jnp.exp(ze - log_exit[p : p + 1]) - jnp.exp(zf - log_final[p : p + 1])
        gap = (gap * exit_scale[p : p + 1]).astype(bf16)
        for j in range(DP):
            out[j, p * TILES : (p + 1) * TILES, :] = gap
    high, rest = split_sum(kl)
    middle = (kl - high).astype(bf16).astype(f32)
    low = kl - high - middle
    lanes = iota((8, 128), 1)
    carried = jnp.where(lanes == 0, high, jnp.where(lanes == 1, middle, jnp.where(lanes == 2, low, 0.0)))
    extra = jnp.concatenate([carried, jnp.zeros((8, 128), f32)], axis=0).astype(bf16)
    for j in range(DP):
        out[j, PAIRS * TILES :, :] = extra


def grad_kernel(gaps, weight, slots, buckets, out, kl_out, hist):
    total = jnp.zeros((LIVE, 512), f32)
    for k in range(BLOCKS):
        rows = [gaps[:, p * TILES + 16 * k : p * TILES + 16 * k + 16, :].astype(f32) for p in range(PAIRS)]
        left = jnp.stack(rows, axis=1).reshape(LIVE, BLOCK).astype(bf16)
        total = total + lax.dot_general(
            left,
            weight[:, k * BLOCK : (k + 1) * BLOCK],
            (((1,), (1,)), ((), ())),
            preferred_element_type=f32,
        )
    pick = slots[...]
    out[...] = lax.dot_general(
        pick.astype(bf16), total.astype(bf16), (((0,), (0,)), ((), ())), preferred_element_type=f32
    ).astype(bf16)
    extra = gaps[:, PAIRS * TILES :, :].astype(f32)[:, :PAIRS, :].reshape(LIVE, 128)
    kl = jnp.sum(extra, axis=1, keepdims=True)
    by_slot = jnp.sum(pick * kl, axis=0, keepdims=True)
    kl_out[...] = jnp.broadcast_to(by_slot, (8, 128))
    mine = jnp.where(iota((8, 128), 1) // XS == iota((8, 128), 0), by_slot, 0.0)
    hot = jnp.where(iota((NB, 128), 0) == buckets[...], 1.0, 0.0)
    hist[...] = lax.dot_general(
        mine,
        hot,
        (((1,), (1,)), ((), ())),
        preferred_element_type=f32,
        precision=lax.Precision.HIGHEST,
    )


def exchange(value, axis):
    return lax.all_to_all(value, axis, 0, 0)


def shards(
    tokens, keep, norm_gain, w_up, w_down, head_gain, w_head, exit_idx, exit_count, kl_bucket
):
    sections = lax.axis_size("section")
    section_id = lax.axis_index("section")
    up_local = pltpu.with_memory_space_constraint(w_up[0], pltpu.VMEM)
    down_local = pltpu.with_memory_space_constraint(w_down[0], pltpu.VMEM)
    head_local = pltpu.with_memory_space_constraint(w_head, pltpu.VMEM)
    keep_mine = lax.dynamic_slice_in_dim(keep, section_id, 1, 0)
    shape = jax.ShapeDtypeStruct
    vmem = pl.BlockSpec(memory_space=pltpu.VMEM)
    current, kept, section_of, slots = call(
        prep_kernel,
        (
            shape((LIVE, 512), bf16),
            shape((LIVE, 128), f32),
            shape((LIVE, 128), f32),
            shape((LIVE, 128), f32),
        ),
        in_specs=[pl.BlockSpec(memory_space=pltpu.SMEM), vmem, vmem, vmem],
        out_specs=[vmem] * 4,
    )(exit_count, exit_idx.reshape(1, -1), keep_mine, tokens)
    mine = current
    for step in range(sections):
        parts = call(
            up_kernel,
            shape((2, NF, HALF, FB + 128), bf16),
            in_specs=[vmem] * 3,
            out_specs=vmem,
        )(current, norm_gain, up_local)
        parts = exchange(parts.reshape(DP, HALF, FB + 128), "dp")
        active = call(
            mid_kernel, shape((DP, HALF, FB), bf16), in_specs=[vmem], out_specs=vmem
        )(parts)
        active = exchange(active, "dp")
        lowered = call(
            down_kernel, shape((LIVE, 512), f32), in_specs=[vmem] * 3, out_specs=vmem
        )(active.reshape(2, NF, HALF, FB), down_local, kept)
        other = lax.ppermute(lowered, "mp", [(0, 1), (1, 0)])
        result = (current.astype(f32) + (lowered + other)).astype(bf16)
        mine = jnp.where(section_id == step, result, mine)
        if step < sections - 1:
            current = lax.ppermute(result, "section", [(i, i + 1) for i in range(sections - 1)])
    zero = jnp.zeros_like(mine)
    own_exit = jnp.where(section_of[:, :1] == section_id.astype(f32), mine, zero)
    own_final = jnp.where(section_id == sections - 1, mine, zero)
    held = jnp.stack([own_exit, own_final])
    spread = held
    for k in range(1, sections):
        spread = spread + lax.ppermute(held, "section", [(i, (i + k) % sections) for i in range(sections)])
    extent = 2 * PAIRS * TILES + 16
    parts = call(
        head_kernel,
        shape((DP, extent, 128), jnp.int16),
        in_specs=[vmem] * 4,
        out_specs=vmem,
        scratch_shapes=[pltpu.VMEM((BLOCKS, 2 * LIVE, BLOCK), f32)],
    )(spread[0], spread[1], head_gain.reshape(1, -1), head_local)
    parts = exchange(parts, "dp")
    logits, stats = call(
        peak_kernel,
        (shape((2 * PAIRS * TILES, 128), f32), shape((8, 8, 128), f32)),
        grid=(DP // SENDERS,),
        in_specs=[pl.BlockSpec((SENDERS, extent, 128), lambda j: (j, 0, 0))],
        out_specs=[
            pl.BlockSpec((2 * PAIRS * TILES, 128), lambda j: (0, 0)),
            pl.BlockSpec((8, 8, 128), lambda j: (0, 0, 0)),
        ],
        scratch_shapes=[pltpu.VMEM((extent, 128), f32)],
    )(parts)
    stats = exchange(stats, ("section", "mp"))
    extent = PAIRS * TILES + 16
    gaps = call(
        gap_kernel, shape((DP, extent, 128), bf16), in_specs=[vmem] * 2, out_specs=vmem
    )(logits, stats)
    gaps = exchange(gaps, "dp")
    feature, kl, hist = call(
        grad_kernel,
        (shape((128, 512), bf16), shape((8, 128), f32), shape((8, NB), f32)),
        in_specs=[vmem] * 4,
        out_specs=[vmem] * 3,
    )(gaps, head_local, slots, kl_bucket.reshape(1, -1))
    feature = exchange(feature.reshape(8, 16, 512), ("section", "mp"))
    feature_grad = jnp.sum(feature.astype(f32), axis=0)
    kl_here = lax.dynamic_slice_in_dim(kl[0], lax.axis_index("dp") * 8, 8, 0)
    return (feature_grad, kl_here, hist[:4])


def solution(mesh):
    return jax.shard_map(
        shards,
        mesh=mesh,
        in_specs=(
            P(None, "dp"),
            P(),
            P("section", "dp"),
            P("section", "dp", "mp"),
            P("section", "mp", "dp"),
            P("dp"),
            P("dp", ("section", "mp")),
            P(),
            P(),
            P(),
        ),
        out_specs=(P(("section", "mp"), "dp"), P("dp"), P()),
        check_vma=False,
    )
```

```python
import jax
import jax.numpy as jnp
from jax import lax
from jax.experimental import pallas as pl
from jax.experimental.pallas import tpu as pltpu
from jax.sharding import PartitionSpec as P

D = 8192
XS = 32
NB = 16
LIVE = 80
DP = 16
PAIRS = LIVE // DP
HALF = LIVE // 2
FB = 896
NF = 8
ROW_TILES = HALF // 8
COL_TILES = FB // 128
COLS = 8192
TILES = COLS // 128
BLOCK = 2048
BLOCKS = COLS // BLOCK
SENDERS = 4
STEPS = 32767.0 / 32768.0
EPS = 1e-05
WEIGHT_COPIES = 4
f32 = jnp.float32
bf16 = jnp.bfloat16
VMEM_LIMIT = 16 * 1024 * 1024


def call(kernel, out_shape, **kw):
    return pl.pallas_call(
        kernel,
        out_shape=out_shape,
        compiler_params=pltpu.CompilerParams(vmem_limit_bytes=VMEM_LIMIT),
        **kw,
    )


def iota(shape, dim):
    return lax.broadcasted_iota(jnp.int32, shape, dim)


def split_sum(column):
    high = column.astype(bf16).astype(f32)
    return high, (column - high).astype(bf16).astype(f32)


def prep_kernel(
    count, index_in, keep_in, buckets_in, tokens_in, gain_in, weight_in,
    rows, kept, planes, exits_here, slots, bucket, gain, weight,
    index, keep, buckets, tokens, small, large,
):
    depth = weight.shape[0] // WEIGHT_COPIES
    copies = [
        pltpu.make_async_copy(weight_in.at[pl.ds(n * depth, depth)], weight.at[pl.ds(n * depth, depth)], large.at[n])
        for n in range(WEIGHT_COPIES)
    ]
    pairs = ((index_in, index), (keep_in, keep), (buckets_in, buckets), (tokens_in, tokens), (gain_in, gain))
    fetches = [pltpu.make_async_copy(*pair, small.at[n]) for n, pair in enumerate(pairs)]
    for copy in fetches + copies:
        copy.start()
    for copy in fetches:
        copy.wait()
    here = lax.axis_index("section")
    lane = iota((1, 4 * XS), 1)
    own = lane // XS
    place = lane % XS
    start = jnp.int32(0)
    position = jnp.full((1, 4 * XS), -1, jnp.int32)
    for s in range(4):
        inside = (own == s) & (place < count[s])
        position = jnp.where(inside, place + start, position)
        start = start + count[s]
    hit = iota((LIVE, 4 * XS), 0) == position
    pick = jnp.where(hit, 1.0, 0.0)
    flat = jnp.concatenate([index[s : s + 1, :] for s in range(4)], axis=1)
    token = jnp.sum(pick * flat.astype(f32), axis=1, keepdims=True).astype(jnp.int32)
    chosen = jnp.where(iota((LIVE, 128), 1) == token, 1.0, 0.0)
    rows[...] = jnp.dot(chosen.astype(bf16), tokens[...], preferred_element_type=f32).astype(bf16)
    flag = jnp.sum(chosen * keep[pl.ds(here, 1), :].astype(f32), axis=1, keepdims=True)
    kept[...] = jnp.broadcast_to(flag, kept.shape)
    planes[...] = jnp.where(iota((8, 128), 0) == here, 1.0, 0.0)
    mine = jnp.sum(jnp.where(own == here, pick, 0.0), axis=1, keepdims=True)
    exits_here[...] = jnp.broadcast_to(mine, exits_here.shape)
    slots[...] = pick
    bucket[...] = jnp.concatenate([buckets[s : s + 1, :] for s in range(4)], axis=1)
    for copy in copies:
        copy.wait()


def up_kernel(state, gain, weight, out):
    wide = state[...].astype(f32)
    normed = (wide * gain[...].astype(f32)).astype(bf16)
    high, low = split_sum(jnp.sum(wide * wide, axis=1, keepdims=True))
    lane = iota((8, 128), 1)
    for t in range(2):
        extra = jnp.zeros((8, 128), f32)
        for r in range(ROW_TILES):
            at = t * HALF + r * 8
            extra = jnp.where(lane == 2 * r, high[at : at + 8], extra)
            extra = jnp.where(lane == 2 * r + 1, low[at : at + 8], extra)
        for f in range(NF):
            out[t * NF + f, ROW_TILES * COL_TILES] = extra.astype(bf16)
    for f in range(NF):
        part = jnp.dot(normed, weight[:, f * FB : (f + 1) * FB], preferred_element_type=f32)
        for t in range(2):
            for r in range(ROW_TILES):
                at = t * HALF + r * 8
                for c in range(COL_TILES):
                    tile = part[at : at + 8, c * 128 : (c + 1) * 128]
                    out[t * NF + f, r * COL_TILES + c] = tile.astype(bf16)


def mid_kernel(parts, out):
    def total(tile):
        value = parts[0, tile].astype(f32)
        for j in range(1, DP):
            value = value + parts[j, tile].astype(f32)
        return value

    squares = total(ROW_TILES * COL_TILES)
    rows = []
    for r in range(ROW_TILES):
        square = squares[:, 2 * r : 2 * r + 1] + squares[:, 2 * r + 1 : 2 * r + 2]
        scale = lax.rsqrt(square / D + EPS)
        tiles = [jax.nn.silu(total(r * COL_TILES + c) * scale) for c in range(COL_TILES)]
        rows.append(jnp.concatenate(tiles, axis=1))
    active = jnp.concatenate(rows, axis=0).astype(bf16)
    for j in range(DP):
        out[j] = active


def down_kernel(active, weight, kept, out):
    total = jnp.zeros((LIVE, 512), f32)
    for f in range(NF):
        both = jnp.concatenate([active[0, f].astype(f32), active[1, f].astype(f32)], axis=0)
        total = total + jnp.dot(
            both.astype(bf16), weight[f * FB : (f + 1) * FB, :], preferred_element_type=f32
        )
    out[...] = total * kept[:, :1]


def finish_kernel(state, lowered, other, first, second, third, planes, exits_here, held):
    result = (state[...].astype(f32) + (lowered[...] + other[...])).astype(bf16)
    mine = jnp.zeros((LIVE, 512), f32)
    for s, value in enumerate((first[...], second[...], third[...], result)):
        mine = mine + value.astype(f32) * planes[s : s + 1, :1]
    held[0] = (mine * exits_here[:, :1]).astype(bf16)
    held[1] = (result.astype(f32) * planes[3:4, :1]).astype(bf16)


def power_above(value):
    return jnp.ceil(jnp.log2(jnp.maximum(value, 1e-30)))


def head_kernel(held, one, two, three, gain, weight, out, parts):
    total = held[...].astype(f32) + one[...].astype(f32) + two[...].astype(f32) + three[...].astype(f32)
    wide = total.reshape(2 * LIVE, 512)
    headed = (wide * gain[...].astype(f32)).astype(bf16)
    peak = jnp.zeros((2 * LIVE, BLOCK), f32)
    for k in range(BLOCKS):
        part = jnp.dot(headed, weight[:, k * BLOCK : (k + 1) * BLOCK], preferred_element_type=f32)
        parts[k] = part
        peak = jnp.maximum(peak, jnp.abs(part))
    power = power_above(jnp.max(peak, axis=1, keepdims=True))
    factor = jnp.exp2(15.0 - power) * STEPS
    for k in range(BLOCKS):
        scaled = jnp.clip(jnp.round(parts[k] * factor), -32767.0, 32767.0)
        tiles = scaled.reshape(2 * LIVE, 16, 128).astype(jnp.int32).astype(jnp.int16)
        for i in range(DP):
            for kind in range(2):
                for p in range(PAIRS):
                    first = (kind * PAIRS + p) * TILES + 16 * k
                    out[i, first : first + 16, :] = tiles[kind * LIVE + i * PAIRS + p]
    squares = jnp.sum(wide * wide, axis=1, keepdims=True)
    square_power = power_above(squares)
    whole = jnp.round(squares * jnp.exp2(29.0 - square_power)).astype(jnp.int32)
    lane = iota((2 * LIVE, 128), 1)
    extra = jnp.where(lane == 0, power.astype(jnp.int32), 0)
    extra = jnp.where(lane == 1, whole >> 15, extra)
    extra = jnp.where(lane == 2, whole & 32767, extra)
    extra = jnp.where(lane == 3, square_power.astype(jnp.int32), extra)
    gap = jnp.zeros((8 - PAIRS, 128), jnp.int32)
    for i in range(DP):
        mine = [extra[kind * LIVE + i * PAIRS : kind * LIVE + (i + 1) * PAIRS] for kind in range(2)]
        rows = jnp.concatenate([mine[0], gap, mine[1], gap], axis=0)
        out[i, 2 * PAIRS * TILES :, :] = rows.astype(jnp.int16)


def peak_kernel(parts, logits, stats, total):
    step = pl.program_id(0)

    @pl.when(step == 0)
    def _():
        total[...] = jnp.zeros_like(total)

    sums = []
    for j in range(SENDERS):
        extra = parts[j, 2 * PAIRS * TILES :, :].astype(jnp.int32).astype(f32)
        factor = jnp.exp2(extra[:, 0:1] - 15.0) * (1.0 / STEPS)
        squares = (extra[:, 1:2] * 32768.0 + extra[:, 2:3]) * jnp.exp2(extra[:, 3:4] - 29.0)
        sums.append((factor, squares))
    for slot in range(2 * PAIRS):
        row = slot // PAIRS * 8 + slot % PAIRS
        first = slot * TILES
        value = total[first : first + TILES, :]
        for j in range(SENDERS):
            whole = parts[j, first : first + TILES, :].astype(jnp.int32).astype(f32)
            value = value + whole * sums[j][0][row : row + 1]
        total[first : first + TILES, :] = value
    extra = total[2 * PAIRS * TILES :, :]
    for j in range(SENDERS):
        extra = extra + sums[j][1]
    total[2 * PAIRS * TILES :, :] = extra

    @pl.when(step == DP // SENDERS - 1)
    def _():
        lane = iota((1, 128), 1)
        for p in range(PAIRS):
            z = []
            for kind in range(2):
                at = 2 * PAIRS * TILES + kind * 8 + p
                scale = lax.rsqrt(total[at : at + 1, :] / D + EPS)
                first = (kind * PAIRS + p) * TILES
                value = total[first : first + TILES, :] * scale
                logits[first : first + TILES, :] = value
                z.append(value)
                if kind == 0:
                    exit_scale = scale
            entries = []
            for value in z:
                peak = jnp.max(jnp.max(value, axis=0, keepdims=True), axis=1, keepdims=True)
                power = jnp.exp(value - peak)
                entries += [peak, jnp.sum(jnp.sum(power, axis=0, keepdims=True), axis=1, keepdims=True)]
            cross = power * (z[1] - z[0])
            entries.append(jnp.sum(jnp.sum(cross, axis=0, keepdims=True), axis=1, keepdims=True))
            entries.append(exit_scale)
            row = jnp.zeros((1, 128), f32)
            for n, entry in enumerate(entries):
                row = jnp.where(lane == n, entry, row)
            for j in range(8):
                stats[j, p : p + 1, :] = row
        for j in range(8):
            stats[j, PAIRS:, :] = jnp.ones((8 - PAIRS, 128), f32)


def gap_kernel(logits, stats, out):
    everyone = stats[...]
    lane = iota((1, 128), 1)
    peaks = jnp.max(everyone, axis=0)
    marks = []
    for column in (0, 2):
        peak = peaks[:, column : column + 1]
        weight = jnp.exp(everyone[:, :, column : column + 1] - peak[None])
        total = jnp.sum(weight * everyone[:, :, column + 1 : column + 2], axis=0)
        marks.append((peak + jnp.log(total), weight, total))
    (log_exit, _, _), (log_final, weight, total) = marks
    cross = jnp.sum(weight * everyone[:, :, 4:5], axis=0)
    kl = cross / total - log_final + log_exit
    exit_scale = peaks[:, 5:6]
    for p in range(PAIRS):
        ze = logits[p * TILES : (p + 1) * TILES, :]
        zf = logits[(PAIRS + p) * TILES : (PAIRS + p + 1) * TILES, :]
        gap = jnp.exp(ze - log_exit[p : p + 1]) - jnp.exp(zf - log_final[p : p + 1])
        gap = (gap * exit_scale[p : p + 1]).astype(bf16)
        for j in range(DP):
            out[j, p * TILES : (p + 1) * TILES, :] = gap
    high, rest = split_sum(kl)
    middle = (kl - high).astype(bf16).astype(f32)
    low = kl - high - middle
    lanes = iota((8, 128), 1)
    carried = jnp.where(lanes == 0, high, jnp.where(lanes == 1, middle, jnp.where(lanes == 2, low, 0.0)))
    extra = jnp.concatenate([carried, jnp.zeros((8, 128), f32)], axis=0).astype(bf16)
    for j in range(DP):
        out[j, PAIRS * TILES :, :] = extra


def grad_kernel(gaps, weight, slots, buckets, out, kl_out, hist):
    total = jnp.zeros((LIVE, 512), f32)
    for k in range(BLOCKS):
        rows = [gaps[:, p * TILES + 16 * k : p * TILES + 16 * k + 16, :].astype(f32) for p in range(PAIRS)]
        left = jnp.stack(rows, axis=1).reshape(LIVE, BLOCK).astype(bf16)
        total = total + lax.dot_general(
            left,
            weight[:, k * BLOCK : (k + 1) * BLOCK],
            (((1,), (1,)), ((), ())),
            preferred_element_type=f32,
        )
    pick = slots[...]
    out[...] = lax.dot_general(
        pick.astype(bf16), total.astype(bf16), (((0,), (0,)), ((), ())), preferred_element_type=f32
    ).astype(bf16)
    extra = gaps[:, PAIRS * TILES :, :].astype(f32)[:, :PAIRS, :].reshape(LIVE, 128)
    kl = jnp.sum(extra, axis=1, keepdims=True)
    by_slot = jnp.sum(pick * kl, axis=0, keepdims=True)
    first = lax.axis_index("dp") * 8
    own = jnp.where(iota((8, 128), 1) == iota((8, 128), 0) + first, 1.0, 0.0)
    kl_out[...] = lax.dot_general(
        by_slot,
        own,
        (((1,), (1,)), ((), ())),
        preferred_element_type=f32,
        precision=lax.Precision.HIGHEST,
    )
    mine = jnp.where(iota((4, 128), 1) // XS == iota((4, 128), 0), by_slot, 0.0)
    hot = jnp.where(iota((NB, 128), 0) == buckets[...], 1.0, 0.0)
    hist[...] = lax.dot_general(
        mine,
        hot,
        (((1,), (1,)), ((), ())),
        preferred_element_type=f32,
        precision=lax.Precision.HIGHEST,
    )


def exchange(value, axis):
    return lax.all_to_all(value, axis, 0, 0)


def around(value, by):
    count = lax.axis_size("section")
    return lax.ppermute(value, "section", [(i, (i + by) % count) for i in range(count)])


def shards(
    tokens, keep, norm_gain, w_up, w_down, head_gain, w_head, exit_idx, exit_count, kl_bucket
):
    sections = lax.axis_size("section")
    down_local = pltpu.with_memory_space_constraint(w_down[0], pltpu.VMEM)
    head_local = pltpu.with_memory_space_constraint(w_head, pltpu.VMEM)
    shape = jax.ShapeDtypeStruct
    vmem = pl.BlockSpec(memory_space=pltpu.VMEM)
    far = pl.BlockSpec(memory_space=pltpu.HBM)
    fetched = (exit_idx, keep, kl_bucket, tokens, norm_gain, w_up[0])
    current, kept, planes, exits_here, slots, bucket, gain, up_local = call(
        prep_kernel,
        (
            shape((LIVE, 512), bf16),
            shape((LIVE, 128), f32),
            shape((8, 128), f32),
            shape((LIVE, 128), f32),
            shape((LIVE, 128), f32),
            shape((1, 128), jnp.int32),
            shape((1, 512), bf16),
            pltpu.VMEM(w_up.shape[1:], bf16),
        ),
        in_specs=[pl.BlockSpec(memory_space=pltpu.SMEM)] + [far] * 6,
        out_specs=[vmem] * 8,
        scratch_shapes=[
            pltpu.VMEM((4, XS), jnp.int32),
            pltpu.VMEM((4, 128), jnp.int32),
            pltpu.VMEM((4, XS), jnp.int32),
            pltpu.VMEM((128, 512), bf16),
            pltpu.SemaphoreType.DMA((5,)),
            pltpu.SemaphoreType.DMA((WEIGHT_COPIES,)),
        ],
    )(exit_count, *[pltpu.with_memory_space_constraint(x, pltpu.HBM) for x in fetched])
    up_local = pltpu.with_memory_space_constraint(up_local, pltpu.VMEM)
    results = []
    for step in range(sections):
        parts = call(
            up_kernel,
            shape((DP, ROW_TILES * COL_TILES + 1, 8, 128), bf16),
            in_specs=[vmem] * 3,
            out_specs=vmem,
        )(current, gain, up_local)
        parts = exchange(parts, "dp")
        active = call(
            mid_kernel, shape((DP, HALF, FB), bf16), in_specs=[vmem], out_specs=vmem
        )(parts)
        active = exchange(active, "dp")
        lowered = call(
            down_kernel, shape((LIVE, 512), f32), in_specs=[vmem] * 3, out_specs=vmem
        )(active.reshape(2, NF, HALF, FB), down_local, kept)
        other = lax.ppermute(lowered, "mp", [(0, 1), (1, 0)])
        if step < sections - 1:
            result = (current.astype(f32) + (lowered + other)).astype(bf16)
            results.append(result)
            current = around(result, 1)
    held = call(
        finish_kernel, shape((2, LIVE, 512), bf16), in_specs=[vmem] * 8, out_specs=vmem
    )(current, lowered, other, *results, planes, exits_here)
    spread = [around(held, k) for k in (2, 1, 3)]
    extent = 2 * PAIRS * TILES + 16
    parts = call(
        head_kernel,
        shape((DP, extent, 128), jnp.int16),
        in_specs=[vmem] * 6,
        out_specs=vmem,
        scratch_shapes=[pltpu.VMEM((BLOCKS, 2 * LIVE, BLOCK), f32)],
    )(held, *spread, head_gain.reshape(1, -1), head_local)
    parts = exchange(parts, "dp")
    logits, stats = call(
        peak_kernel,
        (shape((2 * PAIRS * TILES, 128), f32), shape((8, 8, 128), f32)),
        grid=(DP // SENDERS,),
        in_specs=[pl.BlockSpec((SENDERS, extent, 128), lambda j: (j, 0, 0))],
        out_specs=[
            pl.BlockSpec((2 * PAIRS * TILES, 128), lambda j: (0, 0)),
            pl.BlockSpec((8, 8, 128), lambda j: (0, 0, 0)),
        ],
        scratch_shapes=[pltpu.VMEM((extent, 128), f32)],
    )(parts)
    stats = exchange(stats, ("section", "mp"))
    extent = PAIRS * TILES + 16
    gaps = call(
        gap_kernel, shape((DP, extent, 128), bf16), in_specs=[vmem] * 2, out_specs=vmem
    )(logits, stats)
    gaps = exchange(gaps, "dp")
    feature, kl, hist = call(
        grad_kernel,
        (shape((128, 512), bf16), shape((1, 8), f32), shape((4, NB), f32)),
        in_specs=[vmem] * 4,
        out_specs=[vmem] * 3,
    )(gaps, head_local, slots, bucket)
    feature = exchange(feature.reshape(8, 16, 512), ("section", "mp"))
    feature_grad = jnp.sum(feature.astype(f32), axis=0)
    return (feature_grad, kl.reshape(8), hist)


def solution(mesh):
    return jax.shard_map(
        shards,
        mesh=mesh,
        in_specs=(
            P(None, "dp"),
            P(),
            P("section", "dp"),
            P("section", "dp", "mp"),
            P("section", "mp", "dp"),
            P("dp"),
            P("dp", ("section", "mp")),
            P(),
            P(),
            P(),
        ),
        out_specs=(P(("section", "mp"), "dp"), P("dp"), P()),
        check_vma=False,
    )
```

```python
import functools

import jax
import jax.numpy as jnp
from jax import lax
from jax.experimental import pallas as pl
from jax.experimental.pallas import tpu as pltpu
from jax.sharding import PartitionSpec as P

D = 8192
XS = 32
NB = 16
LIVE = 80
DP = 16
ORDER = (2, 1, 3)
ARRIVAL = (3, 1, 2)
PAIRS = LIVE // DP
QUARTER = 1792
ROW_TILES = LIVE // 8
COL_TILES = QUARTER // 128
TILE_COUNT = ROW_TILES * COL_TILES
COLS = 8192
TILES = COLS // 128
BLOCK = 2048
BLOCKS = COLS // BLOCK
SENDERS = 4
STEPS = 32760.0 / 32768.0
ROUND = 1.5 * 2.0**23
EPS = 1e-05
WEIGHT_COPIES = 4
f32 = jnp.float32
bf16 = jnp.bfloat16
VMEM_LIMIT = 16 * 1024 * 1024


def call(kernel, out_shape, **kw):
    return pl.pallas_call(
        kernel,
        out_shape=out_shape,
        compiler_params=pltpu.CompilerParams(vmem_limit_bytes=VMEM_LIMIT),
        **kw,
    )


def iota(shape, dim):
    return lax.broadcasted_iota(jnp.int32, shape, dim)


def split_sum(column):
    high = column.astype(bf16).astype(f32)
    return high, (column - high).astype(bf16).astype(f32)


def prep_kernel(
    count, index_in, keep_in, buckets_in, tokens_in, gain_in, weight_in,
    rows, kept, planes, slots, bucket, gain, weight,
    index, keep, buckets, tokens, small, large,
):
    depth = weight.shape[0] // WEIGHT_COPIES
    copies = [
        pltpu.make_async_copy(weight_in.at[pl.ds(n * depth, depth)], weight.at[pl.ds(n * depth, depth)], large.at[n])
        for n in range(WEIGHT_COPIES)
    ]
    pairs = ((index_in, index), (keep_in, keep), (buckets_in, buckets), (tokens_in, tokens), (gain_in, gain))
    fetches = [pltpu.make_async_copy(*pair, small.at[n]) for n, pair in enumerate(pairs)]
    for copy in fetches + copies:
        copy.start()
    for copy in fetches:
        copy.wait()
    here = lax.axis_index("section")
    lane = iota((1, 4 * XS), 1)
    own = lane // XS
    place = lane % XS
    start = jnp.int32(0)
    position = jnp.full((1, 4 * XS), -1, jnp.int32)
    for s in range(4):
        inside = (own == s) & (place < count[s])
        position = jnp.where(inside, place + start, position)
        start = start + count[s]
    hit = iota((LIVE, 4 * XS), 0) == position
    pick = jnp.where(hit, 1.0, 0.0)
    flat = jnp.concatenate([index[s : s + 1, :] for s in range(4)], axis=1)
    token = jnp.sum(pick * flat.astype(f32), axis=1, keepdims=True).astype(jnp.int32)
    chosen = jnp.where(iota((LIVE, 128), 1) == token, 1.0, 0.0)
    rows[...] = jnp.dot(chosen.astype(bf16), tokens[...], preferred_element_type=f32).astype(bf16)
    flag = jnp.sum(chosen * keep[pl.ds(here, 1), :].astype(f32), axis=1, keepdims=True)
    kept[...] = jnp.broadcast_to(flag, kept.shape)
    planes[...] = jnp.where(iota((8, 128), 0) == here, 1.0, 0.0)
    slots[...] = pick
    bucket[...] = jnp.concatenate([buckets[s : s + 1, :] for s in range(4)], axis=1)
    for copy in copies:
        copy.wait()


def place_along(first):
    place = lax.axis_index("dp")
    z, y = place // 4, lax.rem(place, 4)
    return jnp.where((lax.axis_index("mp") == 0) == first, y, z)


def quarter_at(shift):
    part = lax.rem(place_along(True) + shift + 4, 4)
    return pl.ds(pl.multiple_of(part * QUARTER, QUARTER), QUARTER)


def carry_squares(column_of, out):
    lane = iota((8, 128), 1)
    extra = jnp.zeros((8, 128), f32)
    for r in range(ROW_TILES):
        high, low = split_sum(column_of(r))
        extra = jnp.where(lane == r, high, jnp.where(lane == 64 + r, low, extra))
    out[TILE_COUNT] = extra.astype(bf16)


def square_of(extra, r):
    return extra[:, r : r + 1] + extra[:, 64 + r : 65 + r]


def up_kernel(shift, state, gain, weight, out):
    wide = state[...].astype(f32)
    squares = jnp.sum(wide * wide, axis=1, keepdims=True)
    carry_squares(lambda r: squares[r * 8 : r * 8 + 8], out)
    normed = (wide * gain[...].astype(f32)).astype(bf16)
    part = jnp.dot(normed, weight[:, quarter_at(shift)], preferred_element_type=f32)
    for r in range(ROW_TILES):
        for c in range(COL_TILES):
            out[r * COL_TILES + c] = part[r * 8 : r * 8 + 8, c * 128 : (c + 1) * 128].astype(bf16)


def add_four(parts, tile):
    value = parts[0][tile].astype(f32)
    for part in parts[1:]:
        value = value + part[tile].astype(f32)
    return value


def sum_kernel(own, one, two, three, out):
    parts = (own, one, two, three)
    for tile in range(TILE_COUNT):
        out[tile] = add_four(parts, tile).astype(bf16)
    extra = add_four(parts, TILE_COUNT)
    carry_squares(lambda r: square_of(extra, r), out)


def mid_kernel(own, one, two, three, out):
    parts = (own, one, two, three)
    extra = add_four(parts, TILE_COUNT)
    rows = []
    for r in range(ROW_TILES):
        scale = lax.rsqrt(square_of(extra, r) / D + EPS)
        tiles = [jax.nn.silu(add_four(parts, r * COL_TILES + c) * scale) for c in range(COL_TILES)]
        rows.append(jnp.concatenate(tiles, axis=1))
    out[...] = jnp.concatenate(rows, axis=0).astype(bf16)


def down_kernel(shift, active, weight, kept, out):
    part = jnp.dot(active[...], weight[quarter_at(-shift), :], preferred_element_type=f32)
    out[...] = part * kept[:, :1]


def down_more_kernel(shift, active, weight, kept, before, out):
    part = jnp.dot(active[...], weight[quarter_at(-shift), :], preferred_element_type=f32)
    out[...] = before[...] + part * kept[:, :1]


def finish_kernel(state, lowered, other, first, second, third, planes, slots, held, spread):
    result = (state[...].astype(f32) + (lowered[...] + other[...])).astype(bf16)
    mine = jnp.zeros((LIVE, 512), f32)
    for s, value in enumerate((first[...], second[...], third[...], result)):
        mine = mine + value.astype(f32) * planes[s : s + 1, :1]
    spread[...] = lax.dot_general(
        slots[...].astype(bf16), mine.astype(bf16), (((0,), (0,)), ((), ())), preferred_element_type=f32
    )
    first_slot = pl.multiple_of(lax.axis_index("section") * XS, XS)
    held[:XS, :] = spread[pl.ds(first_slot, XS), :].astype(bf16)
    held[XS:, :] = (result.astype(f32) * planes[3:4, :1]).astype(bf16)


def power_above(value):
    return jnp.ceil(jnp.log2(jnp.maximum(value, 1e-30)))


def head_kernel(held, one, two, three, slots, gain, weight, out, parts, spread):
    here = lax.axis_index("section")
    finals = jnp.zeros((LIVE, 512), f32)
    for k, source in enumerate((held, one, two, three)):
        plane = lax.rem(here + 4 - k, 4)
        spread[pl.ds(pl.multiple_of(plane * XS, XS), XS), :] = source[:XS, :].astype(f32)
        finals = finals + source[XS:, :].astype(f32)
    exits = jnp.dot(slots[...].astype(bf16), spread[...].astype(bf16), preferred_element_type=f32)
    wide = jnp.concatenate([exits, finals], axis=0)
    headed = (wide * gain[...].astype(f32)).astype(bf16)
    peak = jnp.zeros((2 * LIVE, BLOCK), f32)
    for k in range(BLOCKS):
        part = jnp.dot(headed, weight[:, k * BLOCK : (k + 1) * BLOCK], preferred_element_type=f32)
        parts[k] = part
        peak = jnp.maximum(peak, jnp.abs(part))
    power = power_above(jnp.max(peak, axis=1, keepdims=True))
    factor = jnp.exp2(15.0 - power) * STEPS
    for k in range(BLOCKS):
        scaled = (parts[k] * factor + ROUND) - ROUND
        tiles = scaled.reshape(2 * LIVE, 16, 128).astype(jnp.int32).astype(jnp.int16)
        for i in range(DP):
            for kind in range(2):
                for p in range(PAIRS):
                    first = (kind * PAIRS + p) * TILES + 16 * k
                    out[i, first : first + 16, :] = tiles[kind * LIVE + i * PAIRS + p]
    squares = jnp.sum(wide * wide, axis=1, keepdims=True)
    square_power = power_above(squares)
    whole = jnp.round(squares * jnp.exp2(29.0 - square_power)).astype(jnp.int32)
    lane = iota((2 * LIVE, 128), 1)
    extra = jnp.where(lane == 0, power.astype(jnp.int32), 0)
    extra = jnp.where(lane == 1, whole >> 15, extra)
    extra = jnp.where(lane == 2, whole & 32767, extra)
    extra = jnp.where(lane == 3, square_power.astype(jnp.int32), extra)
    gap = jnp.zeros((8 - PAIRS, 128), jnp.int32)
    for i in range(DP):
        mine = [extra[kind * LIVE + i * PAIRS : kind * LIVE + (i + 1) * PAIRS] for kind in range(2)]
        rows = jnp.concatenate([mine[0], gap, mine[1], gap], axis=0)
        out[i, 2 * PAIRS * TILES :, :] = rows.astype(jnp.int16)


def peak_kernel(parts, logits, stats, total):
    step = pl.program_id(0)

    @pl.when(step == 0)
    def _():
        total[...] = jnp.zeros_like(total)

    sums = []
    for j in range(SENDERS):
        extra = parts[j, 2 * PAIRS * TILES :, :].astype(jnp.int32).astype(f32)
        factor = jnp.exp2(extra[:, 0:1] - 15.0) * (1.0 / STEPS)
        squares = (extra[:, 1:2] * 32768.0 + extra[:, 2:3]) * jnp.exp2(extra[:, 3:4] - 29.0)
        sums.append((factor, squares))
    for slot in range(2 * PAIRS):
        row = slot // PAIRS * 8 + slot % PAIRS
        first = slot * TILES
        value = total[first : first + TILES, :]
        for j in range(SENDERS):
            whole = parts[j, first : first + TILES, :].astype(jnp.int32).astype(f32)
            value = value + whole * sums[j][0][row : row + 1]
        total[first : first + TILES, :] = value
    extra = total[2 * PAIRS * TILES :, :]
    for j in range(SENDERS):
        extra = extra + sums[j][1]
    total[2 * PAIRS * TILES :, :] = extra

    @pl.when(step == DP // SENDERS - 1)
    def _():
        lane = iota((1, 128), 1)
        for p in range(PAIRS):
            z = []
            for kind in range(2):
                at = 2 * PAIRS * TILES + kind * 8 + p
                scale = lax.rsqrt(total[at : at + 1, :] / D + EPS)
                first = (kind * PAIRS + p) * TILES
                value = total[first : first + TILES, :] * scale
                logits[first : first + TILES, :] = value
                z.append(value)
                if kind == 0:
                    exit_scale = scale
            entries = []
            for value in z:
                peak = jnp.max(jnp.max(value, axis=0, keepdims=True), axis=1, keepdims=True)
                power = jnp.exp(value - peak)
                entries += [peak, jnp.sum(jnp.sum(power, axis=0, keepdims=True), axis=1, keepdims=True)]
            cross = power * (z[1] - z[0])
            entries.append(jnp.sum(jnp.sum(cross, axis=0, keepdims=True), axis=1, keepdims=True))
            entries.append(exit_scale)
            row = jnp.zeros((1, 128), f32)
            for n, entry in enumerate(entries):
                row = jnp.where(lane == n, entry, row)
            for j in range(8):
                stats[j, p : p + 1, :] = row
        for j in range(8):
            stats[j, PAIRS:, :] = jnp.ones((8 - PAIRS, 128), f32)


def gap_kernel(logits, stats, out):
    everyone = stats[...]
    lane = iota((1, 128), 1)
    peaks = jnp.max(everyone, axis=0)
    marks = []
    for column in (0, 2):
        peak = peaks[:, column : column + 1]
        weight = jnp.exp(everyone[:, :, column : column + 1] - peak[None])
        total = jnp.sum(weight * everyone[:, :, column + 1 : column + 2], axis=0)
        marks.append((peak + jnp.log(total), weight, total))
    (log_exit, _, _), (log_final, weight, total) = marks
    cross = jnp.sum(weight * everyone[:, :, 4:5], axis=0)
    kl = cross / total - log_final + log_exit
    exit_scale = peaks[:, 5:6]
    for p in range(PAIRS):
        ze = logits[p * TILES : (p + 1) * TILES, :]
        zf = logits[(PAIRS + p) * TILES : (PAIRS + p + 1) * TILES, :]
        gap = jnp.exp(ze - log_exit[p : p + 1]) - jnp.exp(zf - log_final[p : p + 1])
        gap = (gap * exit_scale[p : p + 1]).astype(bf16)
        for j in range(DP):
            out[j, p * TILES : (p + 1) * TILES, :] = gap
    high, rest = split_sum(kl)
    middle = (kl - high).astype(bf16).astype(f32)
    low = kl - high - middle
    lanes = iota((8, 128), 1)
    carried = jnp.where(lanes == 0, high, jnp.where(lanes == 1, middle, jnp.where(lanes == 2, low, 0.0)))
    extra = jnp.concatenate([carried, jnp.zeros((8, 128), f32)], axis=0).astype(bf16)
    for j in range(DP):
        out[j, PAIRS * TILES :, :] = extra


def grad_kernel(gaps, weight, slots, buckets, out, kl_out, hist):
    total = jnp.zeros((LIVE, 512), f32)
    for k in range(BLOCKS):
        rows = [gaps[:, p * TILES + 16 * k : p * TILES + 16 * k + 16, :].astype(f32) for p in range(PAIRS)]
        left = jnp.stack(rows, axis=1).reshape(LIVE, BLOCK).astype(bf16)
        total = total + lax.dot_general(
            left,
            weight[:, k * BLOCK : (k + 1) * BLOCK],
            (((1,), (1,)), ((), ())),
            preferred_element_type=f32,
        )
    pick = slots[...]
    out[...] = lax.dot_general(
        pick.astype(bf16), total.astype(bf16), (((0,), (0,)), ((), ())), preferred_element_type=f32
    ).astype(bf16)
    extra = gaps[:, PAIRS * TILES :, :].astype(f32)[:, :PAIRS, :].reshape(LIVE, 128)
    kl = jnp.sum(extra, axis=1, keepdims=True)
    by_slot = jnp.sum(pick * kl, axis=0, keepdims=True)
    first = lax.axis_index("dp") * 8
    own = jnp.where(iota((8, 128), 1) == iota((8, 128), 0) + first, 1.0, 0.0)
    kl_out[...] = lax.dot_general(
        by_slot,
        own,
        (((1,), (1,)), ((), ())),
        preferred_element_type=f32,
        precision=lax.Precision.HIGHEST,
    )
    mine = jnp.where(iota((4, 128), 1) // XS == iota((4, 128), 0), by_slot, 0.0)
    hot = jnp.where(iota((NB, 128), 0) == buckets[...], 1.0, 0.0)
    hist[...] = lax.dot_general(
        mine,
        hot,
        (((1,), (1,)), ((), ())),
        preferred_element_type=f32,
        precision=lax.Precision.HIGHEST,
    )


def exchange(value, axis):
    return lax.all_to_all(value, axis, 0, 0)


def around_four(value, by, first):
    pairs = []
    for z in range(4):
        for y in range(4):
            for core in range(2):
                to = (z, (y + by) % 4) if (core == 0) == first else ((z + by) % 4, y)
                pairs.append(((z * 4 + y) * 2 + core, (to[0] * 4 + to[1]) * 2 + core))
    return lax.ppermute(value, ("dp", "mp"), pairs)


def around(value, by):
    count = lax.axis_size("section")
    return lax.ppermute(value, "section", [(i, (i + by) % count) for i in range(count)])


def shards(
    tokens, keep, norm_gain, w_up, w_down, head_gain, w_head, exit_idx, exit_count, kl_bucket
):
    sections = lax.axis_size("section")
    down_local = pltpu.with_memory_space_constraint(w_down[0], pltpu.VMEM)
    head_local = pltpu.with_memory_space_constraint(w_head, pltpu.VMEM)
    shape = jax.ShapeDtypeStruct
    vmem = pl.BlockSpec(memory_space=pltpu.VMEM)
    far = pl.BlockSpec(memory_space=pltpu.HBM)
    fetched = (exit_idx, keep, kl_bucket, tokens, norm_gain, w_up[0])
    tiles = shape((TILE_COUNT + 1, 8, 128), bf16)
    current, kept, planes, slots, bucket, gain, up_local = call(
        prep_kernel,
        (
            shape((LIVE, 512), bf16),
            shape((LIVE, 128), f32),
            shape((8, 128), f32),
            shape((LIVE, 128), f32),
            shape((1, 128), jnp.int32),
            shape((1, 512), bf16),
            pltpu.VMEM(w_up.shape[1:], bf16),
        ),
        in_specs=[pl.BlockSpec(memory_space=pltpu.SMEM)] + [far] * 6,
        out_specs=[vmem] * 7,
        scratch_shapes=[
            pltpu.VMEM((4, XS), jnp.int32),
            pltpu.VMEM((4, 128), jnp.int32),
            pltpu.VMEM((4, XS), jnp.int32),
            pltpu.VMEM((128, 512), bf16),
            pltpu.SemaphoreType.DMA((5,)),
            pltpu.SemaphoreType.DMA((WEIGHT_COPIES,)),
        ],
    )(exit_count, *[pltpu.with_memory_space_constraint(x, pltpu.HBM) for x in fetched])
    up_local = pltpu.with_memory_space_constraint(up_local, pltpu.VMEM)
    results = []
    for step in range(sections):
        part, received = {}, {}
        for k in ORDER + (0,):
            part[k] = call(
                functools.partial(up_kernel, k), tiles, in_specs=[vmem] * 3, out_specs=vmem
            )(current, gain, up_local)
            if k:
                received[k] = around_four(part[k], k, True)
        quarter = call(sum_kernel, tiles, in_specs=[vmem] * 4, out_specs=vmem)(
            part[0], *[received[k] for k in ORDER]
        )
        received = {k: around_four(quarter, k, False) for k in ORDER}
        active = call(mid_kernel, shape((LIVE, QUARTER), bf16), in_specs=[vmem] * 4, out_specs=vmem)(
            quarter, *[received[k] for k in ORDER]
        )
        received = {k: around_four(active, k, True) for k in ORDER}
        wide = shape((LIVE, 512), f32)
        lowered = call(
            functools.partial(down_kernel, 0), wide, in_specs=[vmem] * 3, out_specs=vmem
        )(active, down_local, kept)
        for k in ARRIVAL:
            lowered = call(
                functools.partial(down_more_kernel, k), wide, in_specs=[vmem] * 4, out_specs=vmem
            )(received[k], down_local, kept, lowered)
        other = lax.ppermute(lowered, "mp", [(0, 1), (1, 0)])
        if step < sections - 1:
            result = (current.astype(f32) + (lowered + other)).astype(bf16)
            results.append(result)
            current = around(result, 1)
    held = call(
        finish_kernel,
        shape((XS + LIVE, 512), bf16),
        in_specs=[vmem] * 8,
        out_specs=vmem,
        scratch_shapes=[pltpu.VMEM((4 * XS, 512), f32)],
    )(current, lowered, other, *results, planes, slots)
    spread = [around(held, k) for k in (1, 2, 3)]
    extent = 2 * PAIRS * TILES + 16
    parts = call(
        head_kernel,
        shape((DP, extent, 128), jnp.int16),
        in_specs=[vmem] * 7,
        out_specs=vmem,
        scratch_shapes=[pltpu.VMEM((BLOCKS, 2 * LIVE, BLOCK), f32), pltpu.VMEM((4 * XS, 512), f32)],
    )(held, *spread, slots, head_gain.reshape(1, -1), head_local)
    parts = exchange(parts, "dp")
    logits, stats = call(
        peak_kernel,
        (shape((2 * PAIRS * TILES, 128), f32), shape((8, 8, 128), f32)),
        grid=(DP // SENDERS,),
        in_specs=[pl.BlockSpec((SENDERS, extent, 128), lambda j: (j, 0, 0))],
        out_specs=[
            pl.BlockSpec((2 * PAIRS * TILES, 128), lambda j: (0, 0)),
            pl.BlockSpec((8, 8, 128), lambda j: (0, 0, 0)),
        ],
        scratch_shapes=[pltpu.VMEM((extent, 128), f32)],
    )(parts)
    stats = exchange(stats, ("section", "mp"))
    extent = PAIRS * TILES + 16
    gaps = call(
        gap_kernel, shape((DP, extent, 128), bf16), in_specs=[vmem] * 2, out_specs=vmem
    )(logits, stats)
    gaps = exchange(gaps, "dp")
    feature, kl, hist = call(
        grad_kernel,
        (shape((128, 512), bf16), shape((1, 8), f32), shape((4, NB), f32)),
        in_specs=[vmem] * 4,
        out_specs=[vmem] * 3,
    )(gaps, head_local, slots, bucket)
    feature = exchange(feature.reshape(8, 16, 512), ("section", "mp"))
    feature_grad = jnp.sum(feature.astype(f32), axis=0)
    return (feature_grad, kl.reshape(8), hist)


def solution(mesh):
    return jax.shard_map(
        shards,
        mesh=mesh,
        in_specs=(
            P(None, "dp"),
            P(),
            P("section", "dp"),
            P("section", "dp", "mp"),
            P("section", "mp", "dp"),
            P("dp"),
            P("dp", ("section", "mp")),
            P(),
            P(),
            P(),
        ),
        out_specs=(P(("section", "mp"), "dp"), P("dp"), P()),
        check_vma=False,
    )
```

```python
import functools

import jax
import jax.numpy as jnp
from jax import lax
from jax.experimental import pallas as pl
from jax.experimental.pallas import tpu as pltpu
from jax.sharding import PartitionSpec as P

D = 8192
XS = 32
NB = 16
LIVE = 80
DP = 16
ORDER = (2, 1, 3)
ARRIVAL = (3, 1, 2)
PAIRS = LIVE // DP
QUARTER = 1792
ROW_TILES = LIVE // 8
COL_TILES = QUARTER // 128
TILE_COUNT = ROW_TILES * COL_TILES
GROUP = 4 * 2 * PAIRS
COLS = 8192
TILES = COLS // 128
BLOCK = 2048
BLOCKS = COLS // BLOCK
STEPS = 32760.0 / 32768.0
ROUND = 1.5 * 2.0**23
EPS = 1e-05
WEIGHT_COPIES = 4
f32 = jnp.float32
bf16 = jnp.bfloat16
VMEM_LIMIT = 16 * 1024 * 1024


def call(kernel, out_shape, **kw):
    return pl.pallas_call(
        kernel,
        out_shape=out_shape,
        compiler_params=pltpu.CompilerParams(vmem_limit_bytes=VMEM_LIMIT),
        **kw,
    )


def iota(shape, dim):
    return lax.broadcasted_iota(jnp.int32, shape, dim)


def split_sum(column):
    high = column.astype(bf16).astype(f32)
    return high, (column - high).astype(bf16).astype(f32)


def prep_kernel(
    count, index_in, keep_in, buckets_in, tokens_in, gain_in, weight_in,
    rows, kept, planes, slots, bucket, gain, weight,
    index, keep, buckets, tokens, small, large,
):
    depth = weight.shape[0] // WEIGHT_COPIES
    copies = [
        pltpu.make_async_copy(weight_in.at[pl.ds(n * depth, depth)], weight.at[pl.ds(n * depth, depth)], large.at[n])
        for n in range(WEIGHT_COPIES)
    ]
    pairs = ((index_in, index), (keep_in, keep), (buckets_in, buckets), (tokens_in, tokens), (gain_in, gain))
    fetches = [pltpu.make_async_copy(*pair, small.at[n]) for n, pair in enumerate(pairs)]
    for copy in fetches + copies:
        copy.start()
    for copy in fetches:
        copy.wait()
    here = lax.axis_index("section")
    lane = iota((1, 4 * XS), 1)
    own = lane // XS
    place = lane % XS
    start = jnp.int32(0)
    position = jnp.full((1, 4 * XS), -1, jnp.int32)
    for s in range(4):
        inside = (own == s) & (place < count[s])
        position = jnp.where(inside, place + start, position)
        start = start + count[s]
    hit = iota((LIVE, 4 * XS), 0) == position
    pick = jnp.where(hit, 1.0, 0.0)
    flat = jnp.concatenate([index[s : s + 1, :] for s in range(4)], axis=1)
    token = jnp.sum(pick * flat.astype(f32), axis=1, keepdims=True).astype(jnp.int32)
    chosen = jnp.where(iota((LIVE, 128), 1) == token, 1.0, 0.0)
    rows[...] = jnp.dot(chosen.astype(bf16), tokens[...], preferred_element_type=f32).astype(bf16)
    flag = jnp.sum(chosen * keep[pl.ds(here, 1), :].astype(f32), axis=1, keepdims=True)
    kept[...] = jnp.broadcast_to(flag, kept.shape)
    planes[...] = jnp.where(iota((8, 128), 0) == here, 1.0, 0.0)
    slots[...] = pick
    bucket[...] = jnp.concatenate([buckets[s : s + 1, :] for s in range(4)], axis=1)
    for copy in copies:
        copy.wait()


def place_along(first):
    place = lax.axis_index("dp")
    z, y = place // 4, lax.rem(place, 4)
    return jnp.where((lax.axis_index("mp") == 0) == first, y, z)


def quarter_at(shift):
    part = lax.rem(place_along(True) + shift + 4, 4)
    return pl.ds(pl.multiple_of(part * QUARTER, QUARTER), QUARTER)


def carry_squares(column_of, out):
    lane = iota((8, 128), 1)
    extra = jnp.zeros((8, 128), f32)
    for r in range(ROW_TILES):
        high, low = split_sum(column_of(r))
        extra = jnp.where(lane == r, high, jnp.where(lane == 64 + r, low, extra))
    out[TILE_COUNT] = extra.astype(bf16)


def square_of(extra, r):
    return extra[:, r : r + 1] + extra[:, 64 + r : 65 + r]


def up_kernel(shift, state, gain, weight, out):
    wide = state[...].astype(f32)
    squares = jnp.sum(wide * wide, axis=1, keepdims=True)
    carry_squares(lambda r: squares[r * 8 : r * 8 + 8], out)
    normed = (wide * gain[...].astype(f32)).astype(bf16)
    part = jnp.dot(normed, weight[:, quarter_at(shift)], preferred_element_type=f32)
    for r in range(ROW_TILES):
        for c in range(COL_TILES):
            out[r * COL_TILES + c] = part[r * 8 : r * 8 + 8, c * 128 : (c + 1) * 128].astype(bf16)


def add_four(parts, tile):
    value = parts[0][tile].astype(f32)
    for part in parts[1:]:
        value = value + part[tile].astype(f32)
    return value


def sum_kernel(own, one, two, three, out):
    parts = (own, one, two, three)
    for tile in range(TILE_COUNT):
        out[tile] = add_four(parts, tile).astype(bf16)
    extra = add_four(parts, TILE_COUNT)
    carry_squares(lambda r: square_of(extra, r), out)


def mid_kernel(own, one, two, three, out):
    parts = (own, one, two, three)
    extra = add_four(parts, TILE_COUNT)
    rows = []
    for r in range(ROW_TILES):
        scale = lax.rsqrt(square_of(extra, r) / D + EPS)
        tiles = [jax.nn.silu(add_four(parts, r * COL_TILES + c) * scale) for c in range(COL_TILES)]
        rows.append(jnp.concatenate(tiles, axis=1))
    out[...] = jnp.concatenate(rows, axis=0).astype(bf16)


def down_kernel(shift, active, weight, kept, out):
    part = jnp.dot(active[...], weight[quarter_at(-shift), :], preferred_element_type=f32)
    out[...] = part * kept[:, :1]


def down_more_kernel(shift, active, weight, kept, before, out):
    part = jnp.dot(active[...], weight[quarter_at(-shift), :], preferred_element_type=f32)
    out[...] = before[...] + part * kept[:, :1]


def finish_kernel(state, lowered, other, first, second, third, planes, slots, held, spread):
    result = (state[...].astype(f32) + (lowered[...] + other[...])).astype(bf16)
    mine = jnp.zeros((LIVE, 512), f32)
    for s, value in enumerate((first[...], second[...], third[...], result)):
        mine = mine + value.astype(f32) * planes[s : s + 1, :1]
    spread[...] = lax.dot_general(
        slots[...].astype(bf16), mine.astype(bf16), (((0,), (0,)), ((), ())), preferred_element_type=f32
    )
    first_slot = pl.multiple_of(lax.axis_index("section") * XS, XS)
    held[:XS, :] = spread[pl.ds(first_slot, XS), :].astype(bf16)
    held[XS:, :] = (result.astype(f32) * planes[3:4, :1]).astype(bf16)


def power_above(value):
    return jnp.ceil(jnp.log2(jnp.maximum(value, 1e-30)))


def encode_squares(squares, lane, extra):
    power = power_above(squares)
    whole = jnp.round(squares * jnp.exp2(29.0 - power)).astype(jnp.int32)
    extra = jnp.where(lane == 1, whole >> 15, extra)
    extra = jnp.where(lane == 2, whole & 32767, extra)
    return jnp.where(lane == 3, power.astype(jnp.int32), extra)


def decode(extra):
    value = extra.astype(jnp.int32).astype(f32)
    factor = jnp.exp2(value[:, 0:1] - 15.0) * (1.0 / STEPS)
    squares = (value[:, 1:2] * 32768.0 + value[:, 2:3]) * jnp.exp2(value[:, 3:4] - 29.0)
    return factor, squares


def row_of(slot):
    return slot // PAIRS * 8 + slot % PAIRS


def device_at(first, second):
    return jnp.where(lax.axis_index("mp") == 0, second * 4 + first, first * 4 + second)


def head_kernel(held, one, two, three, slots, gain, weight, parts, marks, spread):
    here = lax.axis_index("section")
    finals = jnp.zeros((LIVE, 512), f32)
    for k, source in enumerate((held, one, two, three)):
        plane = lax.rem(here + 4 - k, 4)
        spread[pl.ds(pl.multiple_of(plane * XS, XS), XS), :] = source[:XS, :].astype(f32)
        finals = finals + source[XS:, :].astype(f32)
    exits = jnp.dot(slots[...].astype(bf16), spread[...].astype(bf16), preferred_element_type=f32)
    both = jnp.concatenate([exits, finals], axis=0).astype(bf16)
    row = iota((2 * LIVE, 2 * LIVE), 0)
    slot = lax.rem(row, 2 * PAIRS)
    wanted = slot // PAIRS * LIVE + lax.rem(slot, PAIRS)
    for shift in range(4):
        for second in range(4):
            i = device_at(lax.rem(place_along(True) + shift, 4), second)
            wanted = wanted + jnp.where(row // (2 * PAIRS) == shift * 4 + second, i * PAIRS, 0)
    chosen = jnp.where(iota((2 * LIVE, 2 * LIVE), 1) == wanted, 1.0, 0.0).astype(bf16)
    wide = jnp.dot(chosen, both, preferred_element_type=f32)
    headed = (wide * gain[...].astype(f32)).astype(bf16)
    peak = jnp.zeros((2 * LIVE, BLOCK), f32)
    for k in range(BLOCKS):
        part = jnp.dot(headed, weight[:, k * BLOCK : (k + 1) * BLOCK], preferred_element_type=f32)
        parts[k] = part
        peak = jnp.maximum(peak, jnp.abs(part))
    power = power_above(jnp.max(peak, axis=1, keepdims=True))
    lane = iota((2 * LIVE, 128), 1)
    squares = jnp.sum(wide * wide, axis=1, keepdims=True)
    marks[...] = jnp.where(lane == 0, power, squares)


def code_kernel(shift, parts, marks, out):
    mine = slice(shift * GROUP, (shift + 1) * GROUP)
    power = marks[mine, 0:1]
    factor = jnp.exp2(15.0 - power) * STEPS
    for k in range(BLOCKS):
        scaled = (parts[k, mine, :] * factor + ROUND) - ROUND
        tiles = scaled.reshape(GROUP, 16, 128).astype(jnp.int32).astype(jnp.int16)
        for second in range(4):
            for slot in range(2 * PAIRS):
                first = slot * TILES + 16 * k
                out[second, first : first + 16, :] = tiles[second * 2 * PAIRS + slot]
    lane = iota((GROUP, 128), 1)
    extra = jnp.where(lane == 0, power.astype(jnp.int32), 0)
    extra = encode_squares(marks[mine, 1:2], lane, extra)
    gap = jnp.zeros((8 - PAIRS, 128), jnp.int32)
    for second in range(4):
        at = second * 2 * PAIRS
        rows = jnp.concatenate(
            [extra[at : at + PAIRS], gap, extra[at + PAIRS : at + 2 * PAIRS], gap], axis=0
        )
        out[second, 2 * PAIRS * TILES :, :] = rows.astype(jnp.int16)


def logits_kernel(shift, own, one, two, three, out):
    second = lax.rem(place_along(False) + shift, 4)
    refs = (own, one, two, three)
    codes = [decode(ref[second, 2 * PAIRS * TILES :, :]) for ref in refs]
    lane = iota((16, 128), 1)
    extra = jnp.zeros((16, 128), jnp.int32)
    for slot in range(2 * PAIRS):
        row = row_of(slot)
        first = slot * TILES
        value = jnp.zeros((TILES, 128), f32)
        for ref, (factor, _) in zip(refs, codes):
            whole = ref[second, first : first + TILES, :].astype(jnp.int32).astype(f32)
            value = value + whole * factor[row : row + 1]
        peak = jnp.max(jnp.max(jnp.abs(value), axis=0, keepdims=True), axis=1, keepdims=True)
        power = power_above(peak)
        scaled = (value * (jnp.exp2(15.0 - power) * STEPS) + ROUND) - ROUND
        out[first : first + TILES, :] = scaled.astype(jnp.int32).astype(jnp.int16)
        extra = jnp.where((iota((16, 128), 0) == row) & (lane == 0), power.astype(jnp.int32), extra)
    squares = codes[0][1] + codes[1][1] + codes[2][1] + codes[3][1]
    out[2 * PAIRS * TILES :, :] = encode_squares(squares, lane, extra).astype(jnp.int16)


def peak_kernel(own, one, two, three, logits, stats):
    refs = (own, one, two, three)
    codes = [decode(ref[2 * PAIRS * TILES :, :]) for ref in refs]
    squares = codes[0][1] + codes[1][1] + codes[2][1] + codes[3][1]
    scales = lax.rsqrt(squares / D + EPS)
    lane = iota((1, 128), 1)
    for p in range(PAIRS):
        z = []
        for kind in range(2):
            row = kind * 8 + p
            first = (kind * PAIRS + p) * TILES
            value = jnp.zeros((TILES, 128), f32)
            for ref, (factor, _) in zip(refs, codes):
                whole = ref[first : first + TILES, :].astype(jnp.int32).astype(f32)
                value = value + whole * factor[row : row + 1]
            value = value * scales[row : row + 1]
            logits[first : first + TILES, :] = value
            z.append(value)
        entries = []
        for value in z:
            peak = jnp.max(jnp.max(value, axis=0, keepdims=True), axis=1, keepdims=True)
            power = jnp.exp(value - peak)
            entries += [peak, jnp.sum(jnp.sum(power, axis=0, keepdims=True), axis=1, keepdims=True)]
        cross = power * (z[1] - z[0])
        entries.append(jnp.sum(jnp.sum(cross, axis=0, keepdims=True), axis=1, keepdims=True))
        entries.append(scales[p : p + 1])
        row = jnp.zeros((1, 128), f32)
        for n, entry in enumerate(entries):
            row = jnp.where(lane == n, entry, row)
        stats[p : p + 1, :] = row
    stats[PAIRS:, :] = jnp.ones((8 - PAIRS, 128), f32)


def gap_kernel(logits, own, one, two, three, out, collected):
    here, core = lax.axis_index("section"), lax.axis_index("mp")
    for k, source in enumerate((own, one, two, three)):
        plane = lax.rem(here + 4 - k, 4)
        collected[2 * plane + core] = source[0]
        collected[2 * plane + 1 - core] = source[1]
    everyone = collected[...]
    lane = iota((1, 128), 1)
    peaks = jnp.max(everyone, axis=0)
    marks = []
    for column in (0, 2):
        peak = peaks[:, column : column + 1]
        weight = jnp.exp(everyone[:, :, column : column + 1] - peak[None])
        total = jnp.sum(weight * everyone[:, :, column + 1 : column + 2], axis=0)
        marks.append((peak + jnp.log(total), weight, total))
    (log_exit, _, _), (log_final, weight, total) = marks
    cross = jnp.sum(weight * everyone[:, :, 4:5], axis=0)
    kl = cross / total - log_final + log_exit
    exit_scale = peaks[:, 5:6]
    for p in range(PAIRS):
        ze = logits[p * TILES : (p + 1) * TILES, :]
        zf = logits[(PAIRS + p) * TILES : (PAIRS + p + 1) * TILES, :]
        gap = jnp.exp(ze - log_exit[p : p + 1]) - jnp.exp(zf - log_final[p : p + 1])
        gap = (gap * exit_scale[p : p + 1]).astype(bf16)
        out[p * TILES : (p + 1) * TILES, :] = gap
    high, rest = split_sum(kl)
    middle = (kl - high).astype(bf16).astype(f32)
    low = kl - high - middle
    lanes = iota((8, 128), 1)
    carried = jnp.where(lanes == 0, high, jnp.where(lanes == 1, middle, jnp.where(lanes == 2, low, 0.0)))
    extra = jnp.concatenate([carried, jnp.zeros((8, 128), f32)], axis=0).astype(bf16)
    out[PAIRS * TILES :, :] = extra


def grad_kernel(gaps0, gaps1, gaps2, gaps3, weight, slots, buckets, own, give, kl_out, hist):
    gaps = (gaps0, gaps1, gaps2, gaps3)
    total = jnp.zeros((LIVE, 512), f32)
    for k in range(BLOCKS):
        pieces = []
        for gap in gaps:
            rows = [gap[:, p * TILES + 16 * k : p * TILES + 16 * k + 16, :].astype(f32) for p in range(PAIRS)]
            pieces.append(jnp.stack(rows, axis=1))
        left = jnp.concatenate(pieces, axis=0).reshape(LIVE, BLOCK).astype(bf16)
        total = total + lax.dot_general(
            left,
            weight[:, k * BLOCK : (k + 1) * BLOCK],
            (((1,), (1,)), ((), ())),
            preferred_element_type=f32,
        )
    row = iota((LIVE, LIVE), 0)
    wanted = lax.rem(row, PAIRS)
    for shift in range(4):
        for k in range(4):
            i = device_at(lax.rem(place_along(True) + 4 - shift, 4), lax.rem(place_along(False) + 4 - k, 4))
            wanted = wanted + jnp.where(row // PAIRS == shift * 4 + k, i * PAIRS, 0)
    chosen = jnp.where(iota((LIVE, LIVE), 1) == wanted, 1.0, 0.0).astype(bf16)
    pick = jnp.dot(chosen, slots[...].astype(bf16), preferred_element_type=f32)
    by_slot = lax.dot_general(
        pick.astype(bf16), total.astype(bf16), (((0,), (0,)), ((), ())), preferred_element_type=f32
    ).reshape(4, 2, 16, 512)
    even = lax.axis_index("mp") == 0
    own[...] = jnp.where(even, by_slot[:, 0], by_slot[:, 1])
    give[...] = jnp.where(even, by_slot[:, 1], by_slot[:, 0]).astype(bf16)
    kl = jnp.zeros((1, 128), f32)
    for shift, gap in enumerate(gaps):
        extra = gap[:, PAIRS * TILES :, :].astype(f32)[:, :PAIRS, :].reshape(4 * PAIRS, 128)
        column = jnp.sum(extra, axis=1, keepdims=True)
        first = shift * 4 * PAIRS
        kl = kl + jnp.sum(pick[first : first + 4 * PAIRS] * column, axis=0, keepdims=True)
    first = lax.axis_index("dp") * 8
    rows = jnp.where(iota((8, 128), 1) == iota((8, 128), 0) + first, 1.0, 0.0)
    kl_out[...] = lax.dot_general(
        kl,
        rows,
        (((1,), (1,)), ((), ())),
        preferred_element_type=f32,
        precision=lax.Precision.HIGHEST,
    )
    mine = jnp.where(iota((4, 128), 1) // XS == iota((4, 128), 0), kl, 0.0)
    hot = jnp.where(iota((NB, 128), 0) == buckets[...], 1.0, 0.0)
    hist[...] = lax.dot_general(
        mine,
        hot,
        (((1,), (1,)), ((), ())),
        preferred_element_type=f32,
        precision=lax.Precision.HIGHEST,
    )


def pair_kernel(own, other, out0, out1, out2, out3):
    here = lax.axis_index("section")
    for k, out in enumerate((out0, out1, out2, out3)):
        section = lax.rem(here + k, 4)
        out[...] = (own[section] + other[section].astype(f32)).astype(out.dtype)


def around_four(value, by, first):
    pairs = []
    for z in range(4):
        for y in range(4):
            for core in range(2):
                to = (z, (y + by) % 4) if (core == 0) == first else ((z + by) % 4, y)
                pairs.append(((z * 4 + y) * 2 + core, (to[0] * 4 + to[1]) * 2 + core))
    return lax.ppermute(value, ("dp", "mp"), pairs)


def around(value, by):
    count = lax.axis_size("section")
    return lax.ppermute(value, "section", [(i, (i + by) % count) for i in range(count)])


def shards(
    tokens, keep, norm_gain, w_up, w_down, head_gain, w_head, exit_idx, exit_count, kl_bucket
):
    sections = lax.axis_size("section")
    down_local = pltpu.with_memory_space_constraint(w_down[0], pltpu.VMEM)
    head_local = pltpu.with_memory_space_constraint(w_head, pltpu.VMEM)
    shape = jax.ShapeDtypeStruct
    vmem = pl.BlockSpec(memory_space=pltpu.VMEM)
    far = pl.BlockSpec(memory_space=pltpu.HBM)
    fetched = (exit_idx, keep, kl_bucket, tokens, norm_gain, w_up[0])
    tiles = shape((TILE_COUNT + 1, 8, 128), bf16)
    current, kept, planes, slots, bucket, gain, up_local = call(
        prep_kernel,
        (
            shape((LIVE, 512), bf16),
            shape((LIVE, 128), f32),
            shape((8, 128), f32),
            shape((LIVE, 128), f32),
            shape((1, 128), jnp.int32),
            shape((1, 512), bf16),
            pltpu.VMEM(w_up.shape[1:], bf16),
        ),
        in_specs=[pl.BlockSpec(memory_space=pltpu.SMEM)] + [far] * 6,
        out_specs=[vmem] * 7,
        scratch_shapes=[
            pltpu.VMEM((4, XS), jnp.int32),
            pltpu.VMEM((4, 128), jnp.int32),
            pltpu.VMEM((4, XS), jnp.int32),
            pltpu.VMEM((128, 512), bf16),
            pltpu.SemaphoreType.DMA((5,)),
            pltpu.SemaphoreType.DMA((WEIGHT_COPIES,)),
        ],
    )(exit_count, *[pltpu.with_memory_space_constraint(x, pltpu.HBM) for x in fetched])
    up_local = pltpu.with_memory_space_constraint(up_local, pltpu.VMEM)
    results = []
    for step in range(sections):
        part, received = {}, {}
        for k in ORDER + (0,):
            part[k] = call(
                functools.partial(up_kernel, k), tiles, in_specs=[vmem] * 3, out_specs=vmem
            )(current, gain, up_local)
            if k:
                received[k] = around_four(part[k], k, True)
        quarter = call(sum_kernel, tiles, in_specs=[vmem] * 4, out_specs=vmem)(
            part[0], *[received[k] for k in ORDER]
        )
        received = {k: around_four(quarter, k, False) for k in ORDER}
        active = call(mid_kernel, shape((LIVE, QUARTER), bf16), in_specs=[vmem] * 4, out_specs=vmem)(
            quarter, *[received[k] for k in ORDER]
        )
        received = {k: around_four(active, k, True) for k in ORDER}
        wide = shape((LIVE, 512), f32)
        lowered = call(
            functools.partial(down_kernel, 0), wide, in_specs=[vmem] * 3, out_specs=vmem
        )(active, down_local, kept)
        for k in ARRIVAL:
            lowered = call(
                functools.partial(down_more_kernel, k), wide, in_specs=[vmem] * 4, out_specs=vmem
            )(received[k], down_local, kept, lowered)
        other = lax.ppermute(lowered, "mp", [(0, 1), (1, 0)])
        if step < sections - 1:
            result = (current.astype(f32) + (lowered + other)).astype(bf16)
            results.append(result)
            current = around(result, 1)
    held = call(
        finish_kernel,
        shape((XS + LIVE, 512), bf16),
        in_specs=[vmem] * 8,
        out_specs=vmem,
        scratch_shapes=[pltpu.VMEM((4 * XS, 512), f32)],
    )(current, lowered, other, *results, planes, slots)
    spread = [around(held, k) for k in (1, 2, 3)]
    extent = 2 * PAIRS * TILES + 16
    gain_row = head_gain.reshape(1, -1)
    rows = call(
        head_kernel,
        (shape((BLOCKS, 2 * LIVE, BLOCK), f32), shape((2 * LIVE, 128), f32)),
        in_specs=[vmem] * 7,
        out_specs=[vmem] * 2,
        scratch_shapes=[pltpu.VMEM((4 * XS, 512), f32)],
    )(held, *spread, slots, gain_row, head_local)
    shares = {}
    for k in ORDER + (0,):
        shares[k] = call(
            functools.partial(code_kernel, k),
            shape((4, extent, 128), jnp.int16),
            in_specs=[vmem] * 2,
            out_specs=vmem,
        )(*rows)
        if k:
            shares[k] = around_four(shares[k], k, True)
    shares = [shares[k] for k in (0,) + ORDER]
    part, received = {}, {}
    for k in ORDER + (0,):
        part[k] = call(
            functools.partial(logits_kernel, k),
            shape((extent, 128), jnp.int16),
            in_specs=[vmem] * 4,
            out_specs=vmem,
        )(*shares)
        if k:
            received[k] = around_four(part[k], k, False)
    logits, stats = call(
        peak_kernel,
        (shape((2 * PAIRS * TILES, 128), f32), shape((8, 128), f32)),
        in_specs=[vmem] * 4,
        out_specs=[vmem] * 2,
    )(part[0], *[received[k] for k in ORDER])
    stats = jnp.stack([stats, lax.ppermute(stats, "mp", [(0, 1), (1, 0)])])
    received = {k: around(stats, k) for k in ORDER}
    stats = [stats] + [received[k] for k in (1, 2, 3)]
    extent = PAIRS * TILES + 16
    gaps = call(
        gap_kernel,
        shape((extent, 128), bf16),
        in_specs=[vmem] * 5,
        out_specs=vmem,
        scratch_shapes=[pltpu.VMEM((8, 8, 128), f32)],
    )(logits, *stats)
    received = {k: around_four(gaps, k, False) for k in ORDER}
    gaps = jnp.stack([gaps] + [received[k] for k in (1, 2, 3)])
    received = {k: around_four(gaps, k, True) for k in ORDER}
    own, give, kl, hist = call(
        grad_kernel,
        (
            shape((4, 16, 512), f32),
            shape((4, 16, 512), bf16),
            shape((1, 8), f32),
            shape((4, NB), f32),
        ),
        in_specs=[vmem] * 7,
        out_specs=[vmem] * 4,
    )(gaps, *[received[k] for k in (1, 2, 3)], head_local, slots, bucket)
    other = lax.ppermute(give, "mp", [(0, 1), (1, 0)])
    feature = call(
        pair_kernel,
        (shape((16, 512), f32),) + (shape((16, 512), bf16),) * 3,
        in_specs=[vmem] * 2,
        out_specs=[vmem] * 4,
    )(own, other)
    received = [around(feature[k], k).astype(f32) for k in ORDER]
    feature_grad = feature[0] + received[0] + received[1] + received[2]
    return (feature_grad, kl.reshape(8), hist)


def solution(mesh):
    return jax.shard_map(
        shards,
        mesh=mesh,
        in_specs=(
            P(None, "dp"),
            P(),
            P("section", "dp"),
            P("section", "dp", "mp"),
            P("section", "mp", "dp"),
            P("dp"),
            P("dp", ("section", "mp")),
            P(),
            P(),
            P(),
        ),
        out_specs=(P(("section", "mp"), "dp"), P("dp"), P()),
        check_vma=False,
    )
```

```python
import functools

import jax
import jax.numpy as jnp
from jax import lax
from jax.experimental import pallas as pl
from jax.experimental.pallas import tpu as pltpu
from jax.sharding import PartitionSpec as P

D = 8192
XS = 32
NB = 16
LIVE = 80
DP = 16
ORDER = (2, 1, 3)
ARRIVAL = (3, 1, 2)
PAIRS = LIVE // DP
QUARTER = 1792
ROW_TILES = LIVE // 8
COL_TILES = QUARTER // 128
TILE_COUNT = ROW_TILES * COL_TILES
GROUP = 4 * 2 * PAIRS
COLS = 8192
TILES = COLS // 128
BLOCK = 2048
BLOCKS = COLS // BLOCK
STEPS = 32760.0 / 32768.0
ROUND = 1.5 * 2.0**23
EPS = 1e-05
WEIGHT_COPIES = 4
f32 = jnp.float32
bf16 = jnp.bfloat16
VMEM_LIMIT = 16 * 1024 * 1024


def call(kernel, out_shape, **kw):
    return pl.pallas_call(
        kernel,
        out_shape=out_shape,
        compiler_params=pltpu.CompilerParams(vmem_limit_bytes=VMEM_LIMIT),
        **kw,
    )


def iota(shape, dim):
    return lax.broadcasted_iota(jnp.int32, shape, dim)


def split_sum(column):
    high = column.astype(bf16).astype(f32)
    return high, (column - high).astype(bf16).astype(f32)


def prep_kernel(
    count, index_in, keep_in, buckets_in, tokens_in, gain_in, weight_in,
    rows, kept, planes, slots, bucket, gain, weight,
    index, keep, buckets, tokens, small, large,
):
    depth = weight.shape[0] // WEIGHT_COPIES
    copies = [
        pltpu.make_async_copy(weight_in.at[pl.ds(n * depth, depth)], weight.at[pl.ds(n * depth, depth)], large.at[n])
        for n in range(WEIGHT_COPIES)
    ]
    pairs = ((index_in, index), (keep_in, keep), (buckets_in, buckets), (tokens_in, tokens), (gain_in, gain))
    fetches = [pltpu.make_async_copy(*pair, small.at[n]) for n, pair in enumerate(pairs)]
    for copy in fetches + copies:
        copy.start()
    for copy in fetches:
        copy.wait()
    here = lax.axis_index("section")
    lane = iota((1, 4 * XS), 1)
    own = lane // XS
    place = lane % XS
    start = jnp.int32(0)
    position = jnp.full((1, 4 * XS), -1, jnp.int32)
    for s in range(4):
        inside = (own == s) & (place < count[s])
        position = jnp.where(inside, place + start, position)
        start = start + count[s]
    hit = iota((LIVE, 4 * XS), 0) == position
    pick = jnp.where(hit, 1.0, 0.0)
    flat = jnp.concatenate([index[s : s + 1, :] for s in range(4)], axis=1)
    token = jnp.sum(pick * flat.astype(f32), axis=1, keepdims=True).astype(jnp.int32)
    chosen = jnp.where(iota((LIVE, 128), 1) == token, 1.0, 0.0)
    rows[...] = jnp.dot(chosen.astype(bf16), tokens[...], preferred_element_type=f32).astype(bf16)
    flag = jnp.sum(chosen * keep[pl.ds(here, 1), :].astype(f32), axis=1, keepdims=True)
    kept[...] = jnp.broadcast_to(flag, kept.shape)
    planes[...] = jnp.where(iota((8, 128), 0) == here, 1.0, 0.0)
    slots[...] = pick
    bucket[...] = jnp.concatenate([buckets[s : s + 1, :] for s in range(4)], axis=1)
    for copy in copies:
        copy.wait()


def place_along(first):
    place = lax.axis_index("dp")
    z, y = place // 4, lax.rem(place, 4)
    return jnp.where((lax.axis_index("mp") == 0) == first, y, z)


def quarter_at(shift):
    part = lax.rem(place_along(True) + shift + 4, 4)
    return pl.ds(pl.multiple_of(part * QUARTER, QUARTER), QUARTER)


def carry_squares(column_of, out):
    lane = iota((8, 128), 1)
    extra = jnp.zeros((8, 128), f32)
    for r in range(ROW_TILES):
        high, low = split_sum(column_of(r))
        extra = jnp.where(lane == r, high, jnp.where(lane == 64 + r, low, extra))
    out[TILE_COUNT] = extra.astype(bf16)


def square_of(extra, r):
    return extra[:, r : r + 1] + extra[:, 64 + r : 65 + r]


def up_kernel(shift, state, gain, weight, out):
    wide = state[...].astype(f32)
    squares = jnp.sum(wide * wide, axis=1, keepdims=True)
    carry_squares(lambda r: squares[r * 8 : r * 8 + 8], out)
    normed = (wide * gain[...].astype(f32)).astype(bf16)
    part = jnp.dot(normed, weight[:, quarter_at(shift)], preferred_element_type=f32)
    for r in range(ROW_TILES):
        for c in range(COL_TILES):
            out[r * COL_TILES + c] = part[r * 8 : r * 8 + 8, c * 128 : (c + 1) * 128].astype(bf16)


def add_four(parts, tile):
    value = parts[0][tile].astype(f32)
    for part in parts[1:]:
        value = value + part[tile].astype(f32)
    return value


def sum_kernel(own, one, two, three, out):
    parts = (own, one, two, three)
    for tile in range(TILE_COUNT):
        out[tile] = add_four(parts, tile).astype(bf16)
    extra = add_four(parts, TILE_COUNT)
    carry_squares(lambda r: square_of(extra, r), out)


def mid_kernel(own, one, two, three, out):
    parts = (own, one, two, three)
    extra = add_four(parts, TILE_COUNT)
    rows = []
    for r in range(ROW_TILES):
        scale = lax.rsqrt(square_of(extra, r) / D + EPS)
        tiles = [jax.nn.silu(add_four(parts, r * COL_TILES + c) * scale) for c in range(COL_TILES)]
        rows.append(jnp.concatenate(tiles, axis=1))
    out[...] = jnp.concatenate(rows, axis=0).astype(bf16)


def down_kernel(shift, active, weight, kept, out):
    part = jnp.dot(active[...], weight[quarter_at(-shift), :], preferred_element_type=f32)
    out[...] = part * kept[:, :1]


def down_more_kernel(shift, active, weight, kept, before, out):
    part = jnp.dot(active[...], weight[quarter_at(-shift), :], preferred_element_type=f32)
    out[...] = before[...] + part * kept[:, :1]


def finish_kernel(state, lowered, other, first, second, third, planes, slots, held, spread):
    result = (state[...].astype(f32) + (lowered[...] + other[...])).astype(bf16)
    mine = jnp.zeros((LIVE, 512), f32)
    for s, value in enumerate((first[...], second[...], third[...], result)):
        mine = mine + value.astype(f32) * planes[s : s + 1, :1]
    spread[...] = lax.dot_general(
        slots[...].astype(bf16), mine.astype(bf16), (((0,), (0,)), ((), ())), preferred_element_type=f32
    )
    first_slot = pl.multiple_of(lax.axis_index("section") * XS, XS)
    held[:XS, :] = spread[pl.ds(first_slot, XS), :].astype(bf16)
    held[XS:, :] = (result.astype(f32) * planes[3:4, :1]).astype(bf16)


def power_above(value):
    return jnp.ceil(jnp.log2(jnp.maximum(value, 1e-30)))


def encode_squares(squares, lane, extra):
    power = power_above(squares)
    whole = jnp.round(squares * jnp.exp2(29.0 - power)).astype(jnp.int32)
    extra = jnp.where(lane == 1, whole >> 15, extra)
    extra = jnp.where(lane == 2, whole & 32767, extra)
    return jnp.where(lane == 3, power.astype(jnp.int32), extra)


def decode(extra):
    value = extra.astype(jnp.int32).astype(f32)
    factor = jnp.exp2(value[:, 0:1] - 15.0) * (1.0 / STEPS)
    squares = (value[:, 1:2] * 32768.0 + value[:, 2:3]) * jnp.exp2(value[:, 3:4] - 29.0)
    return factor, squares


def row_of(slot):
    return slot // PAIRS * 8 + slot % PAIRS


def device_at(first, second):
    return jnp.where(lax.axis_index("mp") == 0, second * 4 + first, first * 4 + second)


def head_kernel(held, one, two, three, slots, gain, weight, parts, marks, spread):
    here = lax.axis_index("section")
    finals = jnp.zeros((LIVE, 512), f32)
    for k, source in enumerate((held, one, two, three)):
        plane = lax.rem(here + 4 - k, 4)
        spread[pl.ds(pl.multiple_of(plane * XS, XS), XS), :] = source[:XS, :].astype(f32)
        finals = finals + source[XS:, :].astype(f32)
    exits = jnp.dot(slots[...].astype(bf16), spread[...].astype(bf16), preferred_element_type=f32)
    both = jnp.concatenate([exits, finals], axis=0).astype(bf16)
    row = iota((2 * LIVE, 2 * LIVE), 0)
    slot = lax.rem(row, 2 * PAIRS)
    wanted = slot // PAIRS * LIVE + lax.rem(slot, PAIRS)
    for shift in range(4):
        for second in range(4):
            i = device_at(lax.rem(place_along(True) + shift, 4), second)
            wanted = wanted + jnp.where(row // (2 * PAIRS) == shift * 4 + second, i * PAIRS, 0)
    chosen = jnp.where(iota((2 * LIVE, 2 * LIVE), 1) == wanted, 1.0, 0.0).astype(bf16)
    wide = jnp.dot(chosen, both, preferred_element_type=f32)
    headed = (wide * gain[...].astype(f32)).astype(bf16)
    peak = jnp.zeros((2 * LIVE, BLOCK), f32)
    for k in range(BLOCKS):
        part = jnp.dot(headed, weight[:, k * BLOCK : (k + 1) * BLOCK], preferred_element_type=f32)
        parts[k] = part
        peak = jnp.maximum(peak, jnp.abs(part))
    power = power_above(jnp.max(peak, axis=1, keepdims=True))
    lane = iota((2 * LIVE, 128), 1)
    squares = jnp.sum(wide * wide, axis=1, keepdims=True)
    marks[...] = jnp.where(lane == 0, power, squares)


def code_kernel(shift, parts, marks, out):
    mine = slice(shift * GROUP, (shift + 1) * GROUP)
    power = marks[mine, 0:1]
    factor = jnp.exp2(15.0 - power) * STEPS
    for k in range(BLOCKS):
        scaled = (parts[k, mine, :] * factor + ROUND) - ROUND
        tiles = scaled.reshape(GROUP, 16, 128).astype(jnp.int32).astype(jnp.int16)
        for second in range(4):
            for slot in range(2 * PAIRS):
                first = slot * TILES + 16 * k
                out[second, first : first + 16, :] = tiles[second * 2 * PAIRS + slot]
    lane = iota((GROUP, 128), 1)
    extra = jnp.where(lane == 0, power.astype(jnp.int32), 0)
    extra = encode_squares(marks[mine, 1:2], lane, extra)
    gap = jnp.zeros((8 - PAIRS, 128), jnp.int32)
    for second in range(4):
        at = second * 2 * PAIRS
        rows = jnp.concatenate(
            [extra[at : at + PAIRS], gap, extra[at + PAIRS : at + 2 * PAIRS], gap], axis=0
        )
        out[second, 2 * PAIRS * TILES :, :] = rows.astype(jnp.int16)


def logits_kernel(shift, own, one, two, three, out):
    second = lax.rem(place_along(False) + shift, 4)
    refs = (own, one, two, three)
    codes = [decode(ref[second, 2 * PAIRS * TILES :, :]) for ref in refs]
    lane = iota((16, 128), 1)
    extra = jnp.zeros((16, 128), jnp.int32)
    for slot in range(2 * PAIRS):
        row = row_of(slot)
        first = slot * TILES
        value = jnp.zeros((TILES, 128), f32)
        for ref, (factor, _) in zip(refs, codes):
            whole = ref[second, first : first + TILES, :].astype(jnp.int32).astype(f32)
            value = value + whole * factor[row : row + 1]
        peak = jnp.max(jnp.max(jnp.abs(value), axis=0, keepdims=True), axis=1, keepdims=True)
        power = power_above(peak)
        scaled = (value * (jnp.exp2(15.0 - power) * STEPS) + ROUND) - ROUND
        out[first : first + TILES, :] = scaled.astype(jnp.int32).astype(jnp.int16)
        extra = jnp.where((iota((16, 128), 0) == row) & (lane == 0), power.astype(jnp.int32), extra)
    squares = codes[0][1] + codes[1][1] + codes[2][1] + codes[3][1]
    out[2 * PAIRS * TILES :, :] = encode_squares(squares, lane, extra).astype(jnp.int16)


def peak_kernel(own, one, two, three, logits, stats):
    refs = (own, one, two, three)
    codes = [decode(ref[2 * PAIRS * TILES :, :]) for ref in refs]
    squares = codes[0][1] + codes[1][1] + codes[2][1] + codes[3][1]
    scales = lax.rsqrt(squares / D + EPS)
    lane = iota((1, 128), 1)
    for p in range(PAIRS):
        z = []
        for kind in range(2):
            row = kind * 8 + p
            first = (kind * PAIRS + p) * TILES
            value = jnp.zeros((TILES, 128), f32)
            for ref, (factor, _) in zip(refs, codes):
                whole = ref[first : first + TILES, :].astype(jnp.int32).astype(f32)
                value = value + whole * factor[row : row + 1]
            value = value * scales[row : row + 1]
            logits[first : first + TILES, :] = value
            z.append(value)
        entries = []
        for value in z:
            peak = jnp.max(jnp.max(value, axis=0, keepdims=True), axis=1, keepdims=True)
            power = jnp.exp(value - peak)
            entries += [peak, jnp.sum(jnp.sum(power, axis=0, keepdims=True), axis=1, keepdims=True)]
        cross = power * (z[1] - z[0])
        entries.append(jnp.sum(jnp.sum(cross, axis=0, keepdims=True), axis=1, keepdims=True))
        entries.append(scales[p : p + 1])
        row = jnp.zeros((1, 128), f32)
        for n, entry in enumerate(entries):
            row = jnp.where(lane == n, entry, row)
        stats[p : p + 1, :] = row
    stats[PAIRS:, :] = jnp.ones((8 - PAIRS, 128), f32)


def gap_kernel(logits, own, one, two, three, out, collected):
    here, core = lax.axis_index("section"), lax.axis_index("mp")
    for k, source in enumerate((own, one, two, three)):
        plane = lax.rem(here + 4 - k, 4)
        collected[2 * plane + core] = source[0]
        collected[2 * plane + 1 - core] = source[1]
    everyone = collected[...]
    lane = iota((1, 128), 1)
    peaks = jnp.max(everyone, axis=0)
    marks = []
    for column in (0, 2):
        peak = peaks[:, column : column + 1]
        weight = jnp.exp(everyone[:, :, column : column + 1] - peak[None])
        total = jnp.sum(weight * everyone[:, :, column + 1 : column + 2], axis=0)
        marks.append((peak + jnp.log(total), weight, total))
    (log_exit, _, _), (log_final, weight, total) = marks
    cross = jnp.sum(weight * everyone[:, :, 4:5], axis=0)
    kl = cross / total - log_final + log_exit
    exit_scale = peaks[:, 5:6]
    for p in range(PAIRS):
        ze = logits[p * TILES : (p + 1) * TILES, :]
        zf = logits[(PAIRS + p) * TILES : (PAIRS + p + 1) * TILES, :]
        gap = jnp.exp(ze - log_exit[p : p + 1]) - jnp.exp(zf - log_final[p : p + 1])
        gap = (gap * exit_scale[p : p + 1]).astype(bf16)
        out[p * TILES : (p + 1) * TILES, :] = gap
    high, rest = split_sum(kl)
    middle = (kl - high).astype(bf16).astype(f32)
    low = kl - high - middle
    lanes = iota((8, 128), 1)
    carried = jnp.where(lanes == 0, high, jnp.where(lanes == 1, middle, jnp.where(lanes == 2, low, 0.0)))
    extra = jnp.concatenate([carried, jnp.zeros((8, 128), f32)], axis=0).astype(bf16)
    out[PAIRS * TILES :, :] = extra


def grad_kernel(gaps0, gaps1, gaps2, gaps3, weight, slots, buckets, out, kl_out, hist):
    gaps = (gaps0, gaps1, gaps2, gaps3)
    total = jnp.zeros((LIVE, 512), f32)
    for k in range(BLOCKS):
        pieces = []
        for gap in gaps:
            rows = [gap[:, p * TILES + 16 * k : p * TILES + 16 * k + 16, :].astype(f32) for p in range(PAIRS)]
            pieces.append(jnp.stack(rows, axis=1))
        left = jnp.concatenate(pieces, axis=0).reshape(LIVE, BLOCK).astype(bf16)
        total = total + lax.dot_general(
            left,
            weight[:, k * BLOCK : (k + 1) * BLOCK],
            (((1,), (1,)), ((), ())),
            preferred_element_type=f32,
        )
    row = iota((LIVE, LIVE), 0)
    wanted = lax.rem(row, PAIRS)
    for shift in range(4):
        for k in range(4):
            i = device_at(lax.rem(place_along(True) + 4 - shift, 4), lax.rem(place_along(False) + 4 - k, 4))
            wanted = wanted + jnp.where(row // PAIRS == shift * 4 + k, i * PAIRS, 0)
    chosen = jnp.where(iota((LIVE, LIVE), 1) == wanted, 1.0, 0.0).astype(bf16)
    pick = jnp.dot(chosen, slots[...].astype(bf16), preferred_element_type=f32)
    by_slot = lax.dot_general(
        pick.astype(bf16), total.astype(bf16), (((0,), (0,)), ((), ())), preferred_element_type=f32
    )
    out[...] = by_slot.astype(bf16)
    kl = jnp.zeros((1, 128), f32)
    for shift, gap in enumerate(gaps):
        extra = gap[:, PAIRS * TILES :, :].astype(f32)[:, :PAIRS, :].reshape(4 * PAIRS, 128)
        column = jnp.sum(extra, axis=1, keepdims=True)
        first = shift * 4 * PAIRS
        kl = kl + jnp.sum(pick[first : first + 4 * PAIRS] * column, axis=0, keepdims=True)
    first = lax.axis_index("dp") * 8
    rows = jnp.where(iota((8, 128), 1) == iota((8, 128), 0) + first, 1.0, 0.0)
    kl_out[...] = lax.dot_general(
        kl,
        rows,
        (((1,), (1,)), ((), ())),
        preferred_element_type=f32,
        precision=lax.Precision.HIGHEST,
    )
    mine = jnp.where(iota((4, 128), 1) // XS == iota((4, 128), 0), kl, 0.0)
    hot = jnp.where(iota((NB, 128), 0) == buckets[...], 1.0, 0.0)
    hist[...] = lax.dot_general(
        mine,
        hot,
        (((1,), (1,)), ((), ())),
        preferred_element_type=f32,
        precision=lax.Precision.HIGHEST,
    )


def around_four(value, by, first):
    pairs = []
    for z in range(4):
        for y in range(4):
            for core in range(2):
                to = (z, (y + by) % 4) if (core == 0) == first else ((z + by) % 4, y)
                pairs.append(((z * 4 + y) * 2 + core, (to[0] * 4 + to[1]) * 2 + core))
    return lax.ppermute(value, ("dp", "mp"), pairs)


def around(value, by):
    count = lax.axis_size("section")
    return lax.ppermute(value, "section", [(i, (i + by) % count) for i in range(count)])


def shards(
    tokens, keep, norm_gain, w_up, w_down, head_gain, w_head, exit_idx, exit_count, kl_bucket
):
    sections = lax.axis_size("section")
    down_local = pltpu.with_memory_space_constraint(w_down[0], pltpu.VMEM)
    head_local = pltpu.with_memory_space_constraint(w_head, pltpu.VMEM)
    shape = jax.ShapeDtypeStruct
    vmem = pl.BlockSpec(memory_space=pltpu.VMEM)
    far = pl.BlockSpec(memory_space=pltpu.HBM)
    fetched = (exit_idx, keep, kl_bucket, tokens, norm_gain, w_up[0])
    tiles = shape((TILE_COUNT + 1, 8, 128), bf16)
    current, kept, planes, slots, bucket, gain, up_local = call(
        prep_kernel,
        (
            shape((LIVE, 512), bf16),
            shape((LIVE, 128), f32),
            shape((8, 128), f32),
            shape((LIVE, 128), f32),
            shape((1, 128), jnp.int32),
            shape((1, 512), bf16),
            pltpu.VMEM(w_up.shape[1:], bf16),
        ),
        in_specs=[pl.BlockSpec(memory_space=pltpu.SMEM)] + [far] * 6,
        out_specs=[vmem] * 7,
        scratch_shapes=[
            pltpu.VMEM((4, XS), jnp.int32),
            pltpu.VMEM((4, 128), jnp.int32),
            pltpu.VMEM((4, XS), jnp.int32),
            pltpu.VMEM((128, 512), bf16),
            pltpu.SemaphoreType.DMA((5,)),
            pltpu.SemaphoreType.DMA((WEIGHT_COPIES,)),
        ],
    )(exit_count, *[pltpu.with_memory_space_constraint(x, pltpu.HBM) for x in fetched])
    up_local = pltpu.with_memory_space_constraint(up_local, pltpu.VMEM)
    results = []
    for step in range(sections):
        part, received = {}, {}
        for k in ORDER + (0,):
            part[k] = call(
                functools.partial(up_kernel, k), tiles, in_specs=[vmem] * 3, out_specs=vmem
            )(current, gain, up_local)
            if k:
                received[k] = around_four(part[k], k, True)
        quarter = call(sum_kernel, tiles, in_specs=[vmem] * 4, out_specs=vmem)(
            part[0], *[received[k] for k in ORDER]
        )
        received = {k: around_four(quarter, k, False) for k in ORDER}
        active = call(mid_kernel, shape((LIVE, QUARTER), bf16), in_specs=[vmem] * 4, out_specs=vmem)(
            quarter, *[received[k] for k in ORDER]
        )
        received = {k: around_four(active, k, True) for k in ORDER}
        wide = shape((LIVE, 512), f32)
        lowered = call(
            functools.partial(down_kernel, 0), wide, in_specs=[vmem] * 3, out_specs=vmem
        )(active, down_local, kept)
        for k in ARRIVAL:
            lowered = call(
                functools.partial(down_more_kernel, k), wide, in_specs=[vmem] * 4, out_specs=vmem
            )(received[k], down_local, kept, lowered)
        other = lax.ppermute(lowered, "mp", [(0, 1), (1, 0)])
        if step < sections - 1:
            result = (current.astype(f32) + (lowered + other)).astype(bf16)
            results.append(result)
            current = around(result, 1)
    held = call(
        finish_kernel,
        shape((XS + LIVE, 512), bf16),
        in_specs=[vmem] * 8,
        out_specs=vmem,
        scratch_shapes=[pltpu.VMEM((4 * XS, 512), f32)],
    )(current, lowered, other, *results, planes, slots)
    spread = [around(held, k) for k in (1, 2, 3)]
    extent = 2 * PAIRS * TILES + 16
    gain_row = head_gain.reshape(1, -1)
    rows = call(
        head_kernel,
        (shape((BLOCKS, 2 * LIVE, BLOCK), f32), shape((2 * LIVE, 128), f32)),
        in_specs=[vmem] * 7,
        out_specs=[vmem] * 2,
        scratch_shapes=[pltpu.VMEM((4 * XS, 512), f32)],
    )(held, *spread, slots, gain_row, head_local)
    shares = {}
    for k in ORDER + (0,):
        shares[k] = call(
            functools.partial(code_kernel, k),
            shape((4, extent, 128), jnp.int16),
            in_specs=[vmem] * 2,
            out_specs=vmem,
        )(*rows)
        if k:
            shares[k] = around_four(shares[k], k, True)
    shares = [shares[k] for k in (0,) + ORDER]
    part, received = {}, {}
    for k in ORDER + (0,):
        part[k] = call(
            functools.partial(logits_kernel, k),
            shape((extent, 128), jnp.int16),
            in_specs=[vmem] * 4,
            out_specs=vmem,
        )(*shares)
        if k:
            received[k] = around_four(part[k], k, False)
    logits, stats = call(
        peak_kernel,
        (shape((2 * PAIRS * TILES, 128), f32), shape((8, 128), f32)),
        in_specs=[vmem] * 4,
        out_specs=[vmem] * 2,
    )(part[0], *[received[k] for k in ORDER])
    stats = jnp.stack([stats, lax.ppermute(stats, "mp", [(0, 1), (1, 0)])])
    received = {k: around(stats, k) for k in ORDER}
    stats = [stats] + [received[k] for k in (1, 2, 3)]
    extent = PAIRS * TILES + 16
    gaps = call(
        gap_kernel,
        shape((extent, 128), bf16),
        in_specs=[vmem] * 5,
        out_specs=vmem,
        scratch_shapes=[pltpu.VMEM((8, 8, 128), f32)],
    )(logits, *stats)
    received = {k: around_four(gaps, k, False) for k in ORDER}
    gaps = jnp.stack([gaps] + [received[k] for k in (1, 2, 3)])
    received = {k: around_four(gaps, k, True) for k in ORDER}
    feature, kl, hist = call(
        grad_kernel,
        (shape((128, 512), bf16), shape((1, 8), f32), shape((4, NB), f32)),
        in_specs=[vmem] * 7,
        out_specs=[vmem] * 3,
    )(gaps, *[received[k] for k in (1, 2, 3)], head_local, slots, bucket)
    feature = lax.all_to_all(feature.reshape(8, 16, 512), ("section", "mp"), 0, 0)
    feature_grad = jnp.sum(feature.astype(f32), axis=0)
    return (feature_grad, kl.reshape(8), hist)


def solution(mesh):
    return jax.shard_map(
        shards,
        mesh=mesh,
        in_specs=(
            P(None, "dp"),
            P(),
            P("section", "dp"),
            P("section", "dp", "mp"),
            P("section", "mp", "dp"),
            P("dp"),
            P("dp", ("section", "mp")),
            P(),
            P(),
            P(),
        ),
        out_specs=(P(("section", "mp"), "dp"), P("dp"), P()),
        check_vma=False,
    )
```

```python
import functools

import jax
import jax.numpy as jnp
from jax import lax
from jax.experimental import pallas as pl
from jax.experimental.pallas import tpu as pltpu
from jax.sharding import PartitionSpec as P

D = 8192
XS = 32
NB = 16
LIVE = 80
DP = 16
ORDER = (2, 1, 3)
ARRIVAL = (3, 1, 2)
PAIRS = LIVE // DP
QUARTER = 1792
ROW_TILES = LIVE // 8
COL_TILES = QUARTER // 128
TILE_COUNT = ROW_TILES * COL_TILES
GROUP = 4 * 2 * PAIRS
COLS = 8192
TILES = COLS // 128
BLOCK = 2048
BLOCKS = COLS // BLOCK
STEPS = 32760.0 / 32768.0
ROUND = 1.5 * 2.0**23
EPS = 1e-05
WEIGHT_COPIES = 4
f32 = jnp.float32
bf16 = jnp.bfloat16
VMEM_LIMIT = 16 * 1024 * 1024


def call(kernel, out_shape, **kw):
    return pl.pallas_call(
        kernel,
        out_shape=out_shape,
        compiler_params=pltpu.CompilerParams(vmem_limit_bytes=VMEM_LIMIT),
        **kw,
    )


def iota(shape, dim):
    return lax.broadcasted_iota(jnp.int32, shape, dim)


def split_sum(column):
    high = column.astype(bf16).astype(f32)
    return high, (column - high).astype(bf16).astype(f32)


def prep_kernel(
    count, index_in, keep_in, buckets_in, tokens_in, gain_in, weight_in,
    rows, kept, planes, slots, bucket, gain, weight,
    index, keep, buckets, tokens, small, large,
):
    depth = weight.shape[0] // WEIGHT_COPIES
    copies = [
        pltpu.make_async_copy(weight_in.at[pl.ds(n * depth, depth)], weight.at[pl.ds(n * depth, depth)], large.at[n])
        for n in range(WEIGHT_COPIES)
    ]
    pairs = ((index_in, index), (keep_in, keep), (buckets_in, buckets), (tokens_in, tokens), (gain_in, gain))
    fetches = [pltpu.make_async_copy(*pair, small.at[n]) for n, pair in enumerate(pairs)]
    for copy in fetches + copies:
        copy.start()
    for copy in fetches:
        copy.wait()
    here = lax.axis_index("section")
    lane = iota((1, 4 * XS), 1)
    own = lane // XS
    place = lane % XS
    start = jnp.int32(0)
    position = jnp.full((1, 4 * XS), -1, jnp.int32)
    for s in range(4):
        inside = (own == s) & (place < count[s])
        position = jnp.where(inside, place + start, position)
        start = start + count[s]
    hit = iota((LIVE, 4 * XS), 0) == position
    pick = jnp.where(hit, 1.0, 0.0)
    flat = jnp.concatenate([index[s : s + 1, :] for s in range(4)], axis=1)
    token = jnp.sum(pick * flat.astype(f32), axis=1, keepdims=True).astype(jnp.int32)
    chosen = jnp.where(iota((LIVE, 128), 1) == token, 1.0, 0.0)
    rows[...] = jnp.dot(chosen.astype(bf16), tokens[...], preferred_element_type=f32).astype(bf16)
    flag = jnp.sum(chosen * keep[pl.ds(here, 1), :].astype(f32), axis=1, keepdims=True)
    kept[...] = jnp.broadcast_to(flag, kept.shape)
    planes[...] = jnp.where(iota((8, 128), 0) == here, 1.0, 0.0)
    slots[...] = pick
    bucket[...] = jnp.concatenate([buckets[s : s + 1, :] for s in range(4)], axis=1)
    for copy in copies:
        copy.wait()


def place_along(first):
    place = lax.axis_index("dp")
    z, y = place // 4, lax.rem(place, 4)
    return jnp.where((lax.axis_index("mp") == 0) == first, y, z)


def quarter_at(shift):
    part = lax.rem(place_along(True) + shift + 4, 4)
    return pl.ds(pl.multiple_of(part * QUARTER, QUARTER), QUARTER)


def carry_squares(column_of, out):
    lane = iota((8, 128), 1)
    extra = jnp.zeros((8, 128), f32)
    for r in range(ROW_TILES):
        high, low = split_sum(column_of(r))
        extra = jnp.where(lane == r, high, jnp.where(lane == 64 + r, low, extra))
    out[TILE_COUNT] = extra.astype(bf16)


def square_of(extra, r):
    return extra[:, r : r + 1] + extra[:, 64 + r : 65 + r]


def up_kernel(shift, state, gain, weight, out):
    wide = state[...].astype(f32)
    squares = jnp.sum(wide * wide, axis=1, keepdims=True)
    carry_squares(lambda r: squares[r * 8 : r * 8 + 8], out)
    normed = (wide * gain[...].astype(f32)).astype(bf16)
    part = jnp.dot(normed, weight[:, quarter_at(shift)], preferred_element_type=f32)
    for r in range(ROW_TILES):
        for c in range(COL_TILES):
            out[r * COL_TILES + c] = part[r * 8 : r * 8 + 8, c * 128 : (c + 1) * 128].astype(bf16)


def add_four(parts, tile):
    value = parts[0][tile].astype(f32)
    for part in parts[1:]:
        value = value + part[tile].astype(f32)
    return value


def sum_kernel(own, one, two, three, out):
    parts = (own, one, two, three)
    for tile in range(TILE_COUNT):
        out[tile] = add_four(parts, tile).astype(bf16)
    extra = add_four(parts, TILE_COUNT)
    carry_squares(lambda r: square_of(extra, r), out)


def mid_kernel(own, one, two, three, out):
    parts = (own, one, two, three)
    extra = add_four(parts, TILE_COUNT)
    rows = []
    for r in range(ROW_TILES):
        scale = lax.rsqrt(square_of(extra, r) / D + EPS)
        tiles = [jax.nn.silu(add_four(parts, r * COL_TILES + c) * scale) for c in range(COL_TILES)]
        rows.append(jnp.concatenate(tiles, axis=1))
    out[...] = jnp.concatenate(rows, axis=0).astype(bf16)


def down_kernel(shift, active, weight, kept, out):
    part = jnp.dot(active[...], weight[quarter_at(-shift), :], preferred_element_type=f32)
    out[...] = part * kept[:, :1]


def down_more_kernel(shift, active, weight, kept, before, out):
    part = jnp.dot(active[...], weight[quarter_at(-shift), :], preferred_element_type=f32)
    out[...] = before[...] + part * kept[:, :1]


def finish_kernel(state, lowered, other, first, second, third, planes, slots, held, spread):
    result = (state[...].astype(f32) + (lowered[...] + other[...])).astype(bf16)
    mine = jnp.zeros((LIVE, 512), f32)
    for s, value in enumerate((first[...], second[...], third[...], result)):
        mine = mine + value.astype(f32) * planes[s : s + 1, :1]
    spread[...] = lax.dot_general(
        slots[...].astype(bf16), mine.astype(bf16), (((0,), (0,)), ((), ())), preferred_element_type=f32
    )
    first_slot = pl.multiple_of(lax.axis_index("section") * XS, XS)
    held[:XS, :] = spread[pl.ds(first_slot, XS), :].astype(bf16)
    held[XS:, :] = (result.astype(f32) * planes[3:4, :1]).astype(bf16)


def power_above(value):
    return jnp.ceil(jnp.log2(jnp.maximum(value, 1e-30)))


def encode_squares(squares, lane, extra):
    power = power_above(squares)
    whole = jnp.round(squares * jnp.exp2(29.0 - power)).astype(jnp.int32)
    extra = jnp.where(lane == 1, whole >> 15, extra)
    extra = jnp.where(lane == 2, whole & 32767, extra)
    return jnp.where(lane == 3, power.astype(jnp.int32), extra)


def decode(extra):
    value = extra.astype(jnp.int32).astype(f32)
    factor = jnp.exp2(value[:, 0:1] - 15.0) * (1.0 / STEPS)
    squares = (value[:, 1:2] * 32768.0 + value[:, 2:3]) * jnp.exp2(value[:, 3:4] - 29.0)
    return factor, squares


def row_of(slot):
    return slot // PAIRS * 8 + slot % PAIRS


def device_at(first, second):
    return jnp.where(lax.axis_index("mp") == 0, second * 4 + first, first * 4 + second)


def head_kernel(held, one, two, three, slots, gain, weight, parts, marks, spread):
    here = lax.axis_index("section")
    finals = jnp.zeros((LIVE, 512), f32)
    for k, source in enumerate((held, one, two, three)):
        plane = lax.rem(here + 4 - k, 4)
        spread[pl.ds(pl.multiple_of(plane * XS, XS), XS), :] = source[:XS, :].astype(f32)
        finals = finals + source[XS:, :].astype(f32)
    exits = jnp.dot(slots[...].astype(bf16), spread[...].astype(bf16), preferred_element_type=f32)
    both = jnp.concatenate([exits, finals], axis=0).astype(bf16)
    row = iota((2 * LIVE, 2 * LIVE), 0)
    slot = lax.rem(row, 2 * PAIRS)
    wanted = slot // PAIRS * LIVE + lax.rem(slot, PAIRS)
    for shift in range(4):
        for second in range(4):
            i = device_at(lax.rem(place_along(True) + shift, 4), second)
            wanted = wanted + jnp.where(row // (2 * PAIRS) == shift * 4 + second, i * PAIRS, 0)
    chosen = jnp.where(iota((2 * LIVE, 2 * LIVE), 1) == wanted, 1.0, 0.0).astype(bf16)
    wide = jnp.dot(chosen, both, preferred_element_type=f32)
    headed = (wide * gain[...].astype(f32)).astype(bf16)
    peak = jnp.zeros((2 * LIVE, BLOCK), f32)
    for k in range(BLOCKS):
        part = jnp.dot(headed, weight[:, k * BLOCK : (k + 1) * BLOCK], preferred_element_type=f32)
        parts[k] = part
        peak = jnp.maximum(peak, jnp.abs(part))
    power = power_above(jnp.max(peak, axis=1, keepdims=True))
    lane = iota((2 * LIVE, 128), 1)
    squares = jnp.sum(wide * wide, axis=1, keepdims=True)
    marks[...] = jnp.where(lane == 0, power, squares)


def code_kernel(shift, parts, marks, out):
    mine = slice(shift * GROUP, (shift + 1) * GROUP)
    power = marks[mine, 0:1]
    factor = jnp.exp2(15.0 - power) * STEPS
    for k in range(BLOCKS):
        scaled = (parts[k, mine, :] * factor + ROUND) - ROUND
        tiles = scaled.reshape(GROUP, 16, 128).astype(jnp.int32).astype(jnp.int16)
        for second in range(4):
            for slot in range(2 * PAIRS):
                first = slot * TILES + 16 * k
                out[second, first : first + 16, :] = tiles[second * 2 * PAIRS + slot]
    lane = iota((GROUP, 128), 1)
    extra = jnp.where(lane == 0, power.astype(jnp.int32), 0)
    extra = encode_squares(marks[mine, 1:2], lane, extra)
    gap = jnp.zeros((8 - PAIRS, 128), jnp.int32)
    for second in range(4):
        at = second * 2 * PAIRS
        rows = jnp.concatenate(
            [extra[at : at + PAIRS], gap, extra[at + PAIRS : at + 2 * PAIRS], gap], axis=0
        )
        out[second, 2 * PAIRS * TILES :, :] = rows.astype(jnp.int16)


def logits_kernel(shift, own, one, two, three, out):
    second = lax.rem(place_along(False) + shift, 4)
    refs = (own, one, two, three)
    codes = [decode(ref[second, 2 * PAIRS * TILES :, :]) for ref in refs]
    lane = iota((16, 128), 1)
    extra = jnp.zeros((16, 128), jnp.int32)
    for slot in range(2 * PAIRS):
        row = row_of(slot)
        first = slot * TILES
        value = jnp.zeros((TILES, 128), f32)
        for ref, (factor, _) in zip(refs, codes):
            whole = ref[second, first : first + TILES, :].astype(jnp.int32).astype(f32)
            value = value + whole * factor[row : row + 1]
        peak = jnp.max(jnp.max(jnp.abs(value), axis=0, keepdims=True), axis=1, keepdims=True)
        power = power_above(peak)
        scaled = (value * (jnp.exp2(15.0 - power) * STEPS) + ROUND) - ROUND
        out[first : first + TILES, :] = scaled.astype(jnp.int32).astype(jnp.int16)
        extra = jnp.where((iota((16, 128), 0) == row) & (lane == 0), power.astype(jnp.int32), extra)
    squares = codes[0][1] + codes[1][1] + codes[2][1] + codes[3][1]
    out[2 * PAIRS * TILES :, :] = encode_squares(squares, lane, extra).astype(jnp.int16)


def peak_kernel(own, one, two, three, logits, stats):
    refs = (own, one, two, three)
    codes = [decode(ref[2 * PAIRS * TILES :, :]) for ref in refs]
    squares = codes[0][1] + codes[1][1] + codes[2][1] + codes[3][1]
    scales = lax.rsqrt(squares / D + EPS)
    lane = iota((1, 128), 1)
    for p in range(PAIRS):
        z = []
        for kind in range(2):
            row = kind * 8 + p
            first = (kind * PAIRS + p) * TILES
            value = jnp.zeros((TILES, 128), f32)
            for ref, (factor, _) in zip(refs, codes):
                whole = ref[first : first + TILES, :].astype(jnp.int32).astype(f32)
                value = value + whole * factor[row : row + 1]
            value = value * scales[row : row + 1]
            logits[first : first + TILES, :] = value
            z.append(value)
        entries = []
        for value in z:
            peak = jnp.max(jnp.max(value, axis=0, keepdims=True), axis=1, keepdims=True)
            power = jnp.exp(value - peak)
            entries += [peak, jnp.sum(jnp.sum(power, axis=0, keepdims=True), axis=1, keepdims=True)]
        cross = power * (z[1] - z[0])
        entries.append(jnp.sum(jnp.sum(cross, axis=0, keepdims=True), axis=1, keepdims=True))
        entries.append(scales[p : p + 1])
        row = jnp.zeros((1, 128), f32)
        for n, entry in enumerate(entries):
            row = jnp.where(lane == n, entry, row)
        stats[p : p + 1, :] = row
    stats[PAIRS:, :] = jnp.ones((8 - PAIRS, 128), f32)


def gap_kernel(logits, stats, out):
    everyone = stats[...]
    lane = iota((1, 128), 1)
    peaks = jnp.max(everyone, axis=0)
    marks = []
    for column in (0, 2):
        peak = peaks[:, column : column + 1]
        weight = jnp.exp(everyone[:, :, column : column + 1] - peak[None])
        total = jnp.sum(weight * everyone[:, :, column + 1 : column + 2], axis=0)
        marks.append((peak + jnp.log(total), weight, total))
    (log_exit, _, _), (log_final, weight, total) = marks
    cross = jnp.sum(weight * everyone[:, :, 4:5], axis=0)
    kl = cross / total - log_final + log_exit
    exit_scale = peaks[:, 5:6]
    for p in range(PAIRS):
        ze = logits[p * TILES : (p + 1) * TILES, :]
        zf = logits[(PAIRS + p) * TILES : (PAIRS + p + 1) * TILES, :]
        gap = jnp.exp(ze - log_exit[p : p + 1]) - jnp.exp(zf - log_final[p : p + 1])
        gap = (gap * exit_scale[p : p + 1]).astype(bf16)
        out[p * TILES : (p + 1) * TILES, :] = gap
    high, rest = split_sum(kl)
    middle = (kl - high).astype(bf16).astype(f32)
    low = kl - high - middle
    lanes = iota((8, 128), 1)
    carried = jnp.where(lanes == 0, high, jnp.where(lanes == 1, middle, jnp.where(lanes == 2, low, 0.0)))
    extra = jnp.concatenate([carried, jnp.zeros((8, 128), f32)], axis=0).astype(bf16)
    out[PAIRS * TILES :, :] = extra


def grad_kernel(gaps0, gaps1, gaps2, gaps3, weight, slots, buckets, out, kl_out, hist):
    gaps = (gaps0, gaps1, gaps2, gaps3)
    total = jnp.zeros((LIVE, 512), f32)
    for k in range(BLOCKS):
        pieces = []
        for gap in gaps:
            rows = [gap[:, p * TILES + 16 * k : p * TILES + 16 * k + 16, :].astype(f32) for p in range(PAIRS)]
            pieces.append(jnp.stack(rows, axis=1))
        left = jnp.concatenate(pieces, axis=0).reshape(LIVE, BLOCK).astype(bf16)
        total = total + lax.dot_general(
            left,
            weight[:, k * BLOCK : (k + 1) * BLOCK],
            (((1,), (1,)), ((), ())),
            preferred_element_type=f32,
        )
    row = iota((LIVE, LIVE), 0)
    wanted = lax.rem(row, PAIRS)
    for shift in range(4):
        for k in range(4):
            i = device_at(lax.rem(place_along(True) + 4 - shift, 4), lax.rem(place_along(False) + 4 - k, 4))
            wanted = wanted + jnp.where(row // PAIRS == shift * 4 + k, i * PAIRS, 0)
    chosen = jnp.where(iota((LIVE, LIVE), 1) == wanted, 1.0, 0.0).astype(bf16)
    pick = jnp.dot(chosen, slots[...].astype(bf16), preferred_element_type=f32)
    by_slot = lax.dot_general(
        pick.astype(bf16), total.astype(bf16), (((0,), (0,)), ((), ())), preferred_element_type=f32
    )
    out[...] = by_slot.astype(bf16)
    kl = jnp.zeros((1, 128), f32)
    for shift, gap in enumerate(gaps):
        extra = gap[:, PAIRS * TILES :, :].astype(f32)[:, :PAIRS, :].reshape(4 * PAIRS, 128)
        column = jnp.sum(extra, axis=1, keepdims=True)
        first = shift * 4 * PAIRS
        kl = kl + jnp.sum(pick[first : first + 4 * PAIRS] * column, axis=0, keepdims=True)
    first = lax.axis_index("dp") * 8
    rows = jnp.where(iota((8, 128), 1) == iota((8, 128), 0) + first, 1.0, 0.0)
    kl_out[...] = lax.dot_general(
        kl,
        rows,
        (((1,), (1,)), ((), ())),
        preferred_element_type=f32,
        precision=lax.Precision.HIGHEST,
    )
    mine = jnp.where(iota((4, 128), 1) // XS == iota((4, 128), 0), kl, 0.0)
    hot = jnp.where(iota((NB, 128), 0) == buckets[...], 1.0, 0.0)
    hist[...] = lax.dot_general(
        mine,
        hot,
        (((1,), (1,)), ((), ())),
        preferred_element_type=f32,
        precision=lax.Precision.HIGHEST,
    )


def around_four(value, by, first):
    pairs = []
    for z in range(4):
        for y in range(4):
            for core in range(2):
                to = (z, (y + by) % 4) if (core == 0) == first else ((z + by) % 4, y)
                pairs.append(((z * 4 + y) * 2 + core, (to[0] * 4 + to[1]) * 2 + core))
    return lax.ppermute(value, ("dp", "mp"), pairs)


def around(value, by):
    count = lax.axis_size("section")
    return lax.ppermute(value, "section", [(i, (i + by) % count) for i in range(count)])


def shards(
    tokens, keep, norm_gain, w_up, w_down, head_gain, w_head, exit_idx, exit_count, kl_bucket
):
    sections = lax.axis_size("section")
    down_local = pltpu.with_memory_space_constraint(w_down[0], pltpu.VMEM)
    head_local = pltpu.with_memory_space_constraint(w_head, pltpu.VMEM)
    shape = jax.ShapeDtypeStruct
    vmem = pl.BlockSpec(memory_space=pltpu.VMEM)
    far = pl.BlockSpec(memory_space=pltpu.HBM)
    fetched = (exit_idx, keep, kl_bucket, tokens, norm_gain, w_up[0])
    tiles = shape((TILE_COUNT + 1, 8, 128), bf16)
    current, kept, planes, slots, bucket, gain, up_local = call(
        prep_kernel,
        (
            shape((LIVE, 512), bf16),
            shape((LIVE, 128), f32),
            shape((8, 128), f32),
            shape((LIVE, 128), f32),
            shape((1, 128), jnp.int32),
            shape((1, 512), bf16),
            pltpu.VMEM(w_up.shape[1:], bf16),
        ),
        in_specs=[pl.BlockSpec(memory_space=pltpu.SMEM)] + [far] * 6,
        out_specs=[vmem] * 7,
        scratch_shapes=[
            pltpu.VMEM((4, XS), jnp.int32),
            pltpu.VMEM((4, 128), jnp.int32),
            pltpu.VMEM((4, XS), jnp.int32),
            pltpu.VMEM((128, 512), bf16),
            pltpu.SemaphoreType.DMA((5,)),
            pltpu.SemaphoreType.DMA((WEIGHT_COPIES,)),
        ],
    )(exit_count, *[pltpu.with_memory_space_constraint(x, pltpu.HBM) for x in fetched])
    up_local = pltpu.with_memory_space_constraint(up_local, pltpu.VMEM)
    results = []
    for step in range(sections):
        part, received = {}, {}
        for k in ORDER + (0,):
            part[k] = call(
                functools.partial(up_kernel, k), tiles, in_specs=[vmem] * 3, out_specs=vmem
            )(current, gain, up_local)
            if k:
                received[k] = around_four(part[k], k, True)
        quarter = call(sum_kernel, tiles, in_specs=[vmem] * 4, out_specs=vmem)(
            part[0], *[received[k] for k in ORDER]
        )
        received = {k: around_four(quarter, k, False) for k in ORDER}
        active = call(mid_kernel, shape((LIVE, QUARTER), bf16), in_specs=[vmem] * 4, out_specs=vmem)(
            quarter, *[received[k] for k in ORDER]
        )
        received = {k: around_four(active, k, True) for k in ORDER}
        wide = shape((LIVE, 512), f32)
        lowered = call(
            functools.partial(down_kernel, 0), wide, in_specs=[vmem] * 3, out_specs=vmem
        )(active, down_local, kept)
        for k in ARRIVAL:
            lowered = call(
                functools.partial(down_more_kernel, k), wide, in_specs=[vmem] * 4, out_specs=vmem
            )(received[k], down_local, kept, lowered)
        other = lax.ppermute(lowered, "mp", [(0, 1), (1, 0)])
        if step < sections - 1:
            result = (current.astype(f32) + (lowered + other)).astype(bf16)
            results.append(result)
            current = around(result, 1)
    held = call(
        finish_kernel,
        shape((XS + LIVE, 512), bf16),
        in_specs=[vmem] * 8,
        out_specs=vmem,
        scratch_shapes=[pltpu.VMEM((4 * XS, 512), f32)],
    )(current, lowered, other, *results, planes, slots)
    spread = [around(held, k) for k in (1, 2, 3)]
    extent = 2 * PAIRS * TILES + 16
    gain_row = head_gain.reshape(1, -1)
    rows = call(
        head_kernel,
        (shape((BLOCKS, 2 * LIVE, BLOCK), f32), shape((2 * LIVE, 128), f32)),
        in_specs=[vmem] * 7,
        out_specs=[vmem] * 2,
        scratch_shapes=[pltpu.VMEM((4 * XS, 512), f32)],
    )(held, *spread, slots, gain_row, head_local)
    shares = {}
    for k in ORDER + (0,):
        shares[k] = call(
            functools.partial(code_kernel, k),
            shape((4, extent, 128), jnp.int16),
            in_specs=[vmem] * 2,
            out_specs=vmem,
        )(*rows)
        if k:
            shares[k] = around_four(shares[k], k, True)
    shares = [shares[k] for k in (0,) + ORDER]
    part, received = {}, {}
    for k in ORDER + (0,):
        part[k] = call(
            functools.partial(logits_kernel, k),
            shape((extent, 128), jnp.int16),
            in_specs=[vmem] * 4,
            out_specs=vmem,
        )(*shares)
        if k:
            received[k] = around_four(part[k], k, False)
    logits, stats = call(
        peak_kernel,
        (shape((2 * PAIRS * TILES, 128), f32), shape((8, 128), f32)),
        in_specs=[vmem] * 4,
        out_specs=[vmem] * 2,
    )(part[0], *[received[k] for k in ORDER])
    stats = lax.all_to_all(jnp.broadcast_to(stats[None], (8, 8, 128)), ("section", "mp"), 0, 0)
    extent = PAIRS * TILES + 16
    gaps = call(
        gap_kernel,
        shape((extent, 128), bf16),
        in_specs=[vmem] * 2,
        out_specs=vmem,
    )(logits, stats)
    received = {k: around_four(gaps, k, False) for k in ORDER}
    gaps = jnp.stack([gaps] + [received[k] for k in (1, 2, 3)])
    received = {k: around_four(gaps, k, True) for k in ORDER}
    feature, kl, hist = call(
        grad_kernel,
        (shape((128, 512), bf16), shape((1, 8), f32), shape((4, NB), f32)),
        in_specs=[vmem] * 7,
        out_specs=[vmem] * 3,
    )(gaps, *[received[k] for k in (1, 2, 3)], head_local, slots, bucket)
    feature = lax.all_to_all(feature.reshape(8, 16, 512), ("section", "mp"), 0, 0)
    feature_grad = jnp.sum(feature.astype(f32), axis=0)
    return (feature_grad, kl.reshape(8), hist)


def solution(mesh):
    return jax.shard_map(
        shards,
        mesh=mesh,
        in_specs=(
            P(None, "dp"),
            P(),
            P("section", "dp"),
            P("section", "dp", "mp"),
            P("section", "mp", "dp"),
            P("dp"),
            P("dp", ("section", "mp")),
            P(),
            P(),
            P(),
        ),
        out_specs=(P(("section", "mp"), "dp"), P("dp"), P()),
        check_vma=False,
    )
```
